32 devices in a mesh: chrom: 4 (over y, x), snp: 8 (over z, core).
Axes of the slice: x: 2, y: 2, z: 4, core: 2. Of those that a mesh axis runs over, the one named last changes fastest.
Arguments:
- genotypes: bfloat16 [12288, 16384], P(None, ('chrom', 'snp')), may hold values from 0 to 2, as said below
- probes: bfloat16 [16384, 128], P(('chrom', 'snp')), may hold values from -4 to 4
Outputs:
- unit_basis: float32 [16384, 128], P(('chrom', 'snp'))
- range_log_norms: float32 [128], replicated
The draws below stay inside these ranges and needn't reach their ends.
Inputs may be any that keep to these rules, and one draw needn't show every extreme that they name: `genotypes`: every entry is a dosage 0, 1 or 2.
All inputs are finite; a program needn't handle non-finite values.
Results may differ from the reference program's by a relative error of at most 0.0034.
The reference program's roundings to bfloat16 on the way (of `scaled`, `sketch_high`, `sketch_mid` and `sketch_low`) count: a program that leaves them out, or rounds other values in their place, can miss the bound.
Values sent between devices are 32-bit elements; how exact they have to be, the bound alone decides.
A program may use at most 128 MiB of HBM per device.

```python
import math
import jax
import jax.numpy as jnp
from jax import lax

SAMPLES = 12288
SNP_DEV = 512
PROBES = 128
SNPS = 16384


def draw_genotypes(key, part):
    freq_key = jax.random.fold_in(key, 11)
    first_key = jax.random.fold_in(key, 12)
    second_key = jax.random.fold_in(key, 13)
    position = jnp.arange(SNPS, dtype=jnp.float32) / SNPS
    jitter = jax.random.uniform(freq_key, (SNPS,), jnp.float32, 0.5, 1.0)
    frequency = jnp.exp(jnp.log(0.02) + position * jnp.log(25.0)) * jitter
    frequency = jnp.broadcast_to(frequency[None, :], (SAMPLES, SNPS))
    first_allele = (jax.random.uniform(first_key, (SAMPLES, SNPS), jnp.float32) < frequency).astype(jnp.float32)
    second_allele = (jax.random.uniform(second_key, (SAMPLES, SNPS), jnp.float32) < frequency).astype(jnp.float32)
    return (first_allele + second_allele).astype(jnp.bfloat16)


def draw_probes(key, part):
    shared_key = jax.random.fold_in(key, 21)
    noise_key = jax.random.fold_in(key, 22)
    shared = jnp.clip(jax.random.normal(shared_key, (SNPS, 1), jnp.float32), -4.0, 4.0)
    noise = jax.random.normal(noise_key, (SNPS, PROBES), jnp.float32)
    values = jnp.clip(shared + noise / 56.0, -4.0, 4.0)
    return values.astype(jnp.bfloat16)


def setup_inputs(seed: int = 0) -> dict:
    streams_of = jax.random.split(jax.random.key(seed), 3)
    genotypes = draw_genotypes(jax.random.fold_in(streams_of[2], 71), 0)
    probes = draw_probes(jax.random.fold_in(streams_of[2], 71), 0)
    return {"genotypes": genotypes, "probes": probes}


def standardize(block):
    values = block.astype(jnp.float32)
    column_mean = lax.optimization_barrier(jnp.mean(values, axis=0, keepdims=True))
    centered = values - column_mean
    spread = lax.optimization_barrier(jnp.mean(centered * centered, axis=0, keepdims=True))
    return (centered * (spread + 1e-05) ** (-0.125)).astype(jnp.bfloat16)

def split_parts(sketch):
    sketch_high = lax.optimization_barrier(sketch.astype(jnp.bfloat16))
    remainder = sketch - sketch_high.astype(jnp.float32)
    sketch_mid = lax.optimization_barrier(remainder.astype(jnp.bfloat16))
    sketch_low = (remainder - sketch_mid.astype(jnp.float32)).astype(jnp.bfloat16)
    return jnp.concatenate([sketch_high, sketch_mid, sketch_low], axis=1)

def column_gram(matrix):
    return lax.dot_general(matrix.astype(jnp.float32), matrix.astype(jnp.float32), (((0,), (0,)), ((), ())), precision=lax.Precision.HIGHEST, preferred_element_type=jnp.float32)

def unit_columns(matrix, gram_matrix):
    lower_factor = jnp.linalg.cholesky(gram_matrix)
    return lax.linalg.triangular_solve(lower_factor, matrix, left_side=False, lower=True, transpose_a=True)

def reference(genotypes, probes):
    blocks = SNPS // SNP_DEV
    block_ids = jnp.arange(blocks, dtype=jnp.int32)

    def add_block(running, block_index):
        offset = (block_index * SNP_DEV).astype(jnp.int32)
        columns = lax.dynamic_slice_in_dim(genotypes, offset, SNP_DEV, 1)
        probe_rows = lax.dynamic_slice_in_dim(probes, offset, SNP_DEV, 0)
        scaled = standardize(columns)
        return (running + jnp.dot(scaled.astype(jnp.float32), probe_rows.astype(jnp.float32), preferred_element_type=jnp.float32), None)
    sketch, _ = lax.scan(add_block, jnp.zeros((SAMPLES, PROBES), jnp.float32), block_ids)
    sketch_parts = split_parts(sketch)

    def project(block_index):
        offset = (block_index * SNP_DEV).astype(jnp.int32)
        columns = lax.dynamic_slice_in_dim(genotypes, offset, SNP_DEV, 1)
        scaled = standardize(columns)
        product = lax.dot_general(scaled.astype(jnp.float32), sketch_parts.astype(jnp.float32), (((0,), (0,)), ((), ())), preferred_element_type=jnp.float32)
        return product[:, :PROBES] + product[:, PROBES:2 * PROBES] + product[:, 2 * PROBES:]
    range_rows = lax.map(project, block_ids).reshape(SNPS, PROBES)
    gram_first = column_gram(range_rows)
    range_log_norms = 0.1 * jnp.log(jnp.diagonal(gram_first) / SNPS)
    first_basis = unit_columns(range_rows, gram_first)
    second_basis = unit_columns(first_basis, column_gram(first_basis))
    return (second_basis * math.sqrt(SNPS), range_log_norms)
```

```python
import functools
import math

import jax
import jax.numpy as jnp
from jax import lax
from jax.experimental import pallas as pl
from jax.experimental.pallas import tpu as pltpu
from jax.sharding import PartitionSpec as P

MESH = pl.DeviceIdType.MESH
AXES = ("chrom", "snp")
HIGHEST = lax.Precision.HIGHEST
F32 = jnp.float32
BF16 = jnp.bfloat16


def split_size(size):
    factors = []
    while size > 1:
        factor = 4 if size % 4 == 0 and size > 2 else 2 if size % 2 == 0 else size
        factors.append(factor)
        size //= factor
    return factors


def axis_factors(axis, sizes):
    out, stride = [], 1
    for size in reversed(sizes):
        out.append((axis, stride, size))
        stride *= size
    return out[::-1]


def mesh_factors(chroms, snps):
    halves, rest = [], chroms
    while rest % 2 == 0:
        halves.append(2)
        rest //= 2
    if rest > 1:
        halves.append(rest)
    chrom = axis_factors("chrom", halves)
    core = 2 if snps % 2 == 0 else 1
    snp = [(a, s * core, n) for a, s, n in axis_factors("snp", split_size(snps // core))]
    cores = [("snp", 1, core)] if core > 1 else []
    return cores, chrom, snp


def coordinate(factor):
    axis, stride, size = factor
    return lax.rem(lax.div(lax.axis_index(axis), stride), size)


def peer_id(factor, distance):
    axis, stride, size = factor
    mine = coordinate(factor)
    other = lax.rem(mine + distance, size)
    return tuple(
        lax.axis_index(a) + (other - mine) * stride if a == axis else lax.axis_index(a)
        for a in AXES
    )


def greet(factors):
    barrier = pltpu.get_barrier_semaphore()
    count = 0
    for factor in factors:
        for distance in range(1, factor[2]):
            pl.semaphore_signal(
                barrier, inc=1, device_id=peer_id(factor, distance), device_id_type=MESH
            )
            count += 1
    pl.semaphore_wait(barrier, count)


def rows_of(start, rows):
    return pl.ds(pl.multiple_of(start, 8), rows)


def block_of(rows, most):
    return max(b for b in range(8, most + 1, 8) if rows % b == 0)


class Plan:
    def __init__(self, samples, chroms, snps):
        self.devices = chroms * snps
        per_device = samples // self.devices
        self.pieces = next(q for q in (8, 6, 4, 3, 2, 1) if per_device % (8 * q) == 0)
        self.rows = samples // self.pieces
        self.cores, self.chrom, self.snp = mesh_factors(chroms, snps)
        self.factors = self.cores + self.chrom + self.snp
        self.slots = sum(f[2] - 1 for f in self.factors)

    def order(self, piece):
        turn = piece % max(1, len(self.chrom))
        return self.cores + self.chrom[turn:] + self.chrom[:turn] + self.snp

    def received(self):
        return self.rows


def range_kernel(plan, geno_hbm, probes_ref, range_ref, gram_ref, values, part, full, recv, acc, load_sem, rs_send, rs_recv, ag_send, ag_recv):
    samples, snps = values.shape
    width = probes_ref.shape[1]
    rows, pieces = plan.rows, plan.pieces
    loads = []
    for q in range(pieces):
        piece = pl.ds(q * rows, rows)
        load = pltpu.make_async_copy(geno_hbm.at[piece], values.at[piece], load_sem.at[q])
        load.start()
        loads.append(load)
    greet(plan.factors)

    block = math.gcd(rows, 512)
    zero = jnp.zeros((16, snps), F32)
    sums = (zero, zero)
    for q in range(pieces):
        loads[q].wait()

        def add_block(i, carry, q=q):
            first, second = carry
            start = q * rows + i * block
            one = jnp.zeros((16, snps), BF16)
            two = jnp.zeros((16, snps), BF16)
            for slab in range(block // 16):
                x = values[pl.ds(pl.multiple_of(start + slab * 16, 16), 16), :]
                one = one + x
                two = two + x * x
            return first + one.astype(F32), second + two.astype(F32)

        sums = lax.fori_loop(0, rows // block, add_block, sums)
    total = jnp.sum(sums[0], axis=0, keepdims=True)
    squares = jnp.sum(sums[1], axis=0, keepdims=True)
    mean = total / samples
    whole, square = total.astype(jnp.int32), squares.astype(jnp.int32)
    spread = (square * samples - whole * whole).astype(F32) / float(samples) ** 2
    factor = lax.rsqrt(jnp.sqrt(jnp.sqrt(spread + 1e-05)))
    probes = probes_ref[...]
    acc[...] = jnp.zeros_like(acc)

    tile = math.gcd(rows, 256)

    def sketch_piece(q):
        def one_tile(i, _):
            at = pl.ds(pl.multiple_of(q * rows + i * tile, 16), tile)
            scaled = ((values[at, :].astype(F32) - mean) * factor).astype(BF16)
            values[at, :] = scaled
            part[at, :] = jnp.dot(scaled, probes, preferred_element_type=F32)
            return 0

        lax.fori_loop(0, rows // tile, one_tile, 0)

    bases = []
    for q in range(pieces):
        base, size, path = q * rows, rows, []
        slot, offset = 0, 0
        for factor_ in plan.order(q):
            share = size // factor_[2]
            path.append((factor_, base, share, slot, offset))
            slot += factor_[2] - 1
            offset += (factor_[2] - 1) * share
            base = base + coordinate(factor_) * share
            size = share
        path.append((None, base, size, slot, offset))
        bases.append(path)
    stages = len(plan.factors)
    copies = {}

    def scatter_start(q, s):
        factor_, base, share, slot, offset = bases[q][s]
        sent = []
        for distance in range(1, factor_[2]):
            other = lax.rem(coordinate(factor_) + distance, factor_[2])
            copy = pltpu.make_async_remote_copy(
                src_ref=part.at[rows_of(base + other * share, share)],
                dst_ref=recv.at[q, pl.ds(offset + (distance - 1) * share, share)],
                send_sem=rs_send.at[q, slot + distance - 1],
                recv_sem=rs_recv.at[q, slot + distance - 1],
                device_id=peer_id(factor_, distance),
                device_id_type=MESH,
            )
            copy.start()
            sent.append(copy)
        copies["rs", q, s] = sent

    def scatter_end(q, s):
        factor_, _, share, _, offset = bases[q][s]
        base = bases[q][s + 1][1]
        for copy in copies["rs", q, s]:
            copy.wait_recv()
        step = block_of(share, 64)
        last = s == stages - 1

        def add(i, _):
            at = rows_of(base + i * step, step)
            value = part[at, :]
            for k in range(factor_[2] - 1):
                value = value + recv[q, rows_of(offset + k * share + i * step, step), :]
            if last:
                full[at, :] = value
            else:
                part[at, :] = value
            return 0

        lax.fori_loop(0, share // step, add, 0)

    def gather_start(q, s):
        factor_, _, share, slot, _ = bases[q][s]
        at = rows_of(bases[q][s + 1][1], share)
        sent = []
        for distance in range(1, factor_[2]):
            copy = pltpu.make_async_remote_copy(
                src_ref=full.at[at],
                dst_ref=full.at[at],
                send_sem=ag_send.at[q, slot + distance - 1],
                recv_sem=ag_recv.at[q, slot + distance - 1],
                device_id=peer_id(factor_, distance),
                device_id_type=MESH,
            )
            copy.start()
            sent.append(copy)
        copies["ag", q, s] = sent

    def gather_end(q, s):
        for copy in copies["ag", q, s]:
            copy.wait_recv()

    depth = math.gcd(rows, 768)

    def project(q):
        def one(i, _):
            at = pl.ds(pl.multiple_of(q * rows + i * depth, 16), depth)
            sketch = full[at, :].T
            high = sketch.astype(BF16)
            rest = sketch - high.astype(F32)
            mid = rest.astype(BF16)
            low = (rest - mid.astype(F32)).astype(BF16)
            parts = jnp.concatenate([high, mid, low], axis=0)
            acc[...] += jnp.dot(parts, values[at, :], preferred_element_type=F32)
            return 0

        lax.fori_loop(0, rows // depth, one, 0)

    def step(q, t):
        if t == 0:
            sketch_piece(q)
            if stages:
                scatter_start(q, 0)
            else:
                full[pl.ds(q * rows, rows), :] = part[pl.ds(q * rows, rows), :]
        elif t < stages:
            scatter_end(q, t - 1)
            scatter_start(q, t)
        elif t == stages:
            scatter_end(q, t - 1)
            gather_start(q, stages - 1)
        elif t < 2 * stages:
            gather_end(q, 2 * stages - t)
            gather_start(q, 2 * stages - t - 1)
        else:
            gather_end(q, 0)
            project(q)

    for time in range(pieces + 2 * stages):
        for q in range(pieces):
            if 0 <= time - q <= 2 * stages:
                step(q, time - q)
    for sent in copies.values():
        for copy in sent:
            copy.wait_send()

    result = acc[:width] + acc[width : 2 * width] + acc[2 * width :]
    range_ref[...] = result
    gram_ref[...] = lax.dot_general(
        result, result, (((1,), (1,)), ((), ())), precision=HIGHEST, preferred_element_type=F32
    )


def range_rows(plan, genotypes, probes):
    samples, snps = genotypes.shape
    width = probes.shape[1]
    slots = max(1, plan.slots)
    return pl.pallas_call(
        functools.partial(range_kernel, plan),
        out_shape=(
            jax.ShapeDtypeStruct((width, snps), F32),
            jax.ShapeDtypeStruct((width, width), F32),
        ),
        in_specs=[pl.BlockSpec(memory_space=pl.ANY), pl.BlockSpec(memory_space=pltpu.VMEM)],
        out_specs=[pl.BlockSpec(memory_space=pltpu.VMEM)] * 2,
        scratch_shapes=[
            pltpu.VMEM((samples, snps), BF16),
            pltpu.VMEM((samples, width), F32),
            pltpu.VMEM((samples, width), F32),
            pltpu.VMEM((plan.pieces, plan.rows, width), F32),
            pltpu.VMEM((3 * width, snps), F32),
            pltpu.SemaphoreType.DMA((plan.pieces,)),
            pltpu.SemaphoreType.DMA((plan.pieces, slots)),
            pltpu.SemaphoreType.DMA((plan.pieces, slots)),
            pltpu.SemaphoreType.DMA((plan.pieces, slots)),
            pltpu.SemaphoreType.DMA((plan.pieces, slots)),
        ],
        compiler_params=pltpu.CompilerParams(
            collective_id=0, has_side_effects=True, vmem_limit_bytes=48 * 1024 * 1024
        ),
        name="range_rows",
    )(genotypes, probes)


def basis_kernel(last, gram_ref, rows_ref, out_ref, gram_out_ref, work):
    width = gram_ref.shape[0]
    row = lax.broadcasted_iota(jnp.int32, (width, width), 0)
    lane = lax.broadcasted_iota(jnp.int32, (width, width), 1)
    work[:, :width] = gram_ref[...]
    work[:, width:] = jnp.where(row == lane, 1.0, 0.0).astype(F32)
    sub = lax.broadcasted_iota(jnp.int32, (8, width), 0)
    lanes = lax.broadcasted_iota(jnp.int32, (8, width), 1)
    for k in range(0, width, 8):
        left, right = work[k : k + 8, :width], work[k : k + 8, width:]
        columns = [jnp.broadcast_to(left[:, k + j : k + j + 1], (8, width)) for j in range(8)]
        scale = jnp.zeros((8, width), F32)
        for j in range(8):
            pivot = jnp.broadcast_to(columns[j][j : j + 1, :], (8, width))
            root = lax.rsqrt(pivot)
            scale = jnp.where(sub == j, root, scale)
            if j < 7:
                ratio = jnp.where(sub > j, columns[j] / pivot, 0.0)
                left = left - ratio * jnp.broadcast_to(left[j : j + 1, :], (8, width))
                right = right - ratio * jnp.broadcast_to(right[j : j + 1, :], (8, width))
                for m in range(j + 1, 8):
                    columns[m] = columns[m] - ratio * jnp.broadcast_to(columns[m][j : j + 1, :], (8, width))
        left, right = left * scale, right * scale
        work[k : k + 8, :width] = left
        work[k : k + 8, width:] = right
        if k + 8 < width:
            coefficients = jnp.where(lanes >= k + 8, left, 0.0).T
            panel = jnp.concatenate([left, right], axis=1)
            update = jnp.dot(coefficients[k + 8 :], panel, precision=HIGHEST, preferred_element_type=F32)
            work[k + 8 :, :] -= update
    inverse = jnp.where(row >= lane, work[:, width:], 0.0)
    basis = jnp.dot(inverse, rows_ref[...], precision=HIGHEST, preferred_element_type=F32)
    if last is None:
        out_ref[...] = basis
        gram_out_ref[...] = lax.dot_general(
            basis, basis, (((1,), (1,)), ((), ())), precision=HIGHEST, preferred_element_type=F32
        )
    else:
        out_ref[...] = (basis * last).T
        gram_out_ref[...] = gram_ref[...]


def basis_of(gram, rows, last=None):
    width, snps = rows.shape
    shape = (width, snps) if last is None else (snps, width)
    return pl.pallas_call(
        functools.partial(basis_kernel, last),
        out_shape=(jax.ShapeDtypeStruct(shape, F32), jax.ShapeDtypeStruct((width, width), F32)),
        in_specs=[pl.BlockSpec(memory_space=pltpu.VMEM)] * 2,
        out_specs=[pl.BlockSpec(memory_space=pltpu.VMEM)] * 2,
        scratch_shapes=[pltpu.VMEM((width, 2 * width), F32)],
        name="basis",
    )(gram, rows)


def body(chroms, snps, genotypes, probes):
    plan = Plan(genotypes.shape[0], chroms, snps)
    rows, partial_gram = range_rows(plan, genotypes, probes)
    total_snps = rows.shape[1] * chroms * snps
    gram_first = lax.psum(partial_gram, AXES)
    range_log_norms = 0.1 * jnp.log(jnp.diagonal(gram_first) / total_snps)
    first_basis, partial_gram = basis_of(gram_first, rows)
    gram_second = lax.psum(partial_gram, AXES)
    unit_basis, _ = basis_of(gram_second, first_basis, math.sqrt(total_snps))
    return unit_basis, range_log_norms


def solution(mesh):
    return jax.shard_map(
        functools.partial(body, mesh.shape["chrom"], mesh.shape["snp"]),
        mesh=mesh,
        in_specs=(P(None, AXES), P(AXES, None)),
        out_specs=(P(AXES, None), P()),
        check_vma=False,
    )
```

```python
import functools
import itertools
import math

import jax
import jax.numpy as jnp
from jax import lax
from jax.experimental import pallas as pl
from jax.experimental.pallas import tpu as pltpu
from jax.sharding import PartitionSpec as P

MESH = pl.DeviceIdType.MESH
AXES = ("chrom", "snp")
HIGHEST = lax.Precision.HIGHEST
F32 = jnp.float32
BF16 = jnp.bfloat16


def split_size(size):
    factors = []
    while size > 1:
        factor = 4 if size % 4 == 0 and size > 2 else 2 if size % 2 == 0 else size
        factors.append(factor)
        size //= factor
    return factors


def axis_factors(axis, sizes):
    out, stride = [], 1
    for size in reversed(sizes):
        out.append((axis, stride, size))
        stride *= size
    return out[::-1]


def mesh_factors(chroms, snps):
    halves, rest = [], chroms
    while rest % 2 == 0:
        halves.append(2)
        rest //= 2
    if rest > 1:
        halves.append(rest)
    chrom = axis_factors("chrom", halves)
    core = 2 if snps % 2 == 0 else 1
    snp = [(a, s * core, n) for a, s, n in axis_factors("snp", split_size(snps // core))]
    cores = [("snp", 1, core)] if core > 1 else []
    return cores, chrom, snp


def coordinate(factor):
    axis, stride, size = factor
    return lax.rem(lax.div(lax.axis_index(axis), stride), size)


def peer_id(factor, distance):
    axis, stride, size = factor
    mine = coordinate(factor)
    other = lax.rem(mine + distance, size)
    return tuple(
        lax.axis_index(a) + (other - mine) * stride if a == axis else lax.axis_index(a)
        for a in AXES
    )


def near_peer(plan, steps):
    ids = {a: lax.axis_index(a) for a in AXES}
    place = 0
    for (axis, stride, size), step in zip(plan.near, steps):
        mine = coordinate((axis, stride, size))
        other = lax.rem(mine + step, size)
        ids[axis] = ids[axis] + (other - mine) * stride
        place = place * size + other
    return tuple(ids[a] for a in AXES), place


def greet(plan):
    barrier = pltpu.get_barrier_semaphore()
    peers = [near_peer(plan, steps)[0] for steps in plan.near_steps]
    for factor in plan.snp:
        peers += [peer_id(factor, distance) for distance in range(1, factor[2])]
    for peer in peers:
        pl.semaphore_signal(barrier, inc=1, device_id=peer, device_id_type=MESH)
    pl.semaphore_wait(barrier, len(peers))


def sum_gram(plan, turn, gram, near, far, sems):
    near_send, near_recv, far_send, far_recv, back_send, back_recv = sems
    share = gram.shape[0] // plan.near_size
    _, me = near_peer(plan, [0] * len(plan.near))
    mine = rows_of(me * share, share)
    copies = []
    for i, steps in enumerate(plan.near_steps):
        peer, place = near_peer(plan, steps)
        copy = pltpu.make_async_remote_copy(
            src_ref=gram.at[rows_of(place * share, share)],
            dst_ref=near.at[turn, i],
            send_sem=near_send.at[turn, i],
            recv_sem=near_recv.at[turn, i],
            device_id=peer,
            device_id_type=MESH,
        )
        copy.start()
        copies.append(copy)
    value = gram[mine, :]
    for i, copy in enumerate(copies):
        copy.wait_recv()
        value = value + near[turn, i]
    pending = list(copies)
    slot, first = 0, 0
    for factor in plan.snp:
        size = factor[2]
        place = first + coordinate(factor)
        far[turn, place] = value
        copies = []
        for distance in range(1, size):
            copy = pltpu.make_async_remote_copy(
                src_ref=far.at[turn, place],
                dst_ref=far.at[turn, place],
                send_sem=far_send.at[turn, slot],
                recv_sem=far_recv.at[turn, slot],
                device_id=peer_id(factor, distance),
                device_id_type=MESH,
            )
            copy.start()
            copies.append(copy)
            slot += 1
        for copy in copies:
            copy.wait_recv()
        value = far[turn, first]
        for k in range(1, size):
            value = value + far[turn, first + k]
        first += size
        pending += copies
    for copy in pending:
        copy.wait_send()
    return value, me, share


def spread_gram(plan, turn, value, me, share, total, sems):
    mine = rows_of(me * share, share)
    total[turn, mine, :] = value
    copies = []
    for i, steps in enumerate(plan.near_steps):
        peer, _ = near_peer(plan, steps)
        copy = pltpu.make_async_remote_copy(
            src_ref=total.at[turn, mine],
            dst_ref=total.at[turn, mine],
            send_sem=sems[4].at[turn, i],
            recv_sem=sems[5].at[turn, i],
            device_id=peer,
            device_id_type=MESH,
        )
        copy.start()
        copies.append(copy)
    for copy in copies:
        copy.wait_recv()
    for copy in copies:
        copy.wait_send()


def rows_of(start, rows):
    return pl.ds(pl.multiple_of(start, 8), rows)


def block_of(rows, most):
    return max(b for b in range(8, most + 1, 8) if rows % b == 0)


class Plan:
    def __init__(self, samples, chroms, snps):
        self.devices = chroms * snps
        per_device = samples // self.devices
        self.pieces = next(q for q in (16, 12, 8, 6, 4, 3, 2, 1) if per_device % (8 * q) == 0)
        self.rows = samples // self.pieces
        self.cores, self.chrom, self.snp = mesh_factors(chroms, snps)
        self.factors = self.cores + self.chrom + self.snp
        self.slots = sum(f[2] - 1 for f in self.factors)
        self.lanes = max(1, len(self.chrom)) if self.pieces % max(1, len(self.chrom)) == 0 else 1
        near = self.cores + [("chrom", 1, chroms)]
        self.near = [f for f in near if f[2] > 1]
        self.near_size = math.prod(f[2] for f in self.near)
        self.near_steps = list(itertools.product(*[range(f[2]) for f in self.near]))[1:]
        self.far_slots = sum(f[2] - 1 for f in self.snp)
        self.far_size = sum(f[2] for f in self.snp)

    def order(self, piece):
        turn = piece % max(1, len(self.chrom))
        return self.cores + self.chrom[turn:] + self.chrom[:turn] + self.snp


def range_kernel(plan, geno_hbm, probes_ref, out_ref, norms_ref, values, part, full, recv, acc, gram, near, far, grams, work, load_sem, rs_send, rs_recv, ag_send, ag_recv, *sems):
    samples, snps = values.shape
    width = probes_ref.shape[1]
    rows, pieces = plan.rows, plan.pieces
    loads = []
    for q in range(pieces):
        piece = pl.ds(q * rows, rows)
        load = pltpu.make_async_copy(geno_hbm.at[piece], values.at[piece], load_sem.at[q])
        load.start()
        loads.append(load)
    greet(plan)

    block = math.gcd(rows, 512)
    zero = jnp.zeros((16, snps), F32)
    sums = (zero, zero)
    for q in range(pieces):
        loads[q].wait()

        def add_block(i, carry, q=q):
            first, second = carry
            start = q * rows + i * block
            one = jnp.zeros((16, snps), BF16)
            two = jnp.zeros((16, snps), BF16)
            for slab in range(block // 16):
                x = values[pl.ds(pl.multiple_of(start + slab * 16, 16), 16), :]
                one = one + x
                two = two + x * x
            return first + one.astype(F32), second + two.astype(F32)

        sums = lax.fori_loop(0, rows // block, add_block, sums)
    total = jnp.sum(sums[0], axis=0, keepdims=True)
    squares = jnp.sum(sums[1], axis=0, keepdims=True)
    mean = total / samples
    whole, square = total.astype(jnp.int32), squares.astype(jnp.int32)
    spread = (square * samples - whole * whole).astype(F32) / float(samples) ** 2
    factor = lax.rsqrt(jnp.sqrt(jnp.sqrt(spread + 1e-05)))
    probes = probes_ref[...]
    acc[...] = jnp.zeros_like(acc)

    tile = math.gcd(rows, 256)

    def sketch_piece(q):
        def one_tile(i, _):
            at = pl.ds(pl.multiple_of(q * rows + i * tile, 16), tile)
            scaled = ((values[at, :].astype(F32) - mean) * factor).astype(BF16)
            values[at, :] = scaled
            part[at, :] = jnp.dot(scaled, probes, preferred_element_type=F32)
            return 0

        lax.fori_loop(0, rows // tile, one_tile, 0)

    bases = []
    for q in range(pieces):
        base, size, path = q * rows, rows, []
        slot, offset = 0, 0
        for factor_ in plan.order(q):
            share = size // factor_[2]
            path.append((factor_, base, share, slot, offset))
            slot += factor_[2] - 1
            offset += (factor_[2] - 1) * share
            base = base + coordinate(factor_) * share
            size = share
        path.append((None, base, size, slot, offset))
        bases.append(path)
    stages = len(plan.factors)
    copies = {}

    def scatter_start(q, s):
        factor_, base, share, slot, offset = bases[q][s]
        sent = []
        for distance in range(1, factor_[2]):
            other = lax.rem(coordinate(factor_) + distance, factor_[2])
            copy = pltpu.make_async_remote_copy(
                src_ref=part.at[rows_of(base + other * share, share)],
                dst_ref=recv.at[q, pl.ds(offset + (distance - 1) * share, share)],
                send_sem=rs_send.at[q, slot + distance - 1],
                recv_sem=rs_recv.at[q, slot + distance - 1],
                device_id=peer_id(factor_, distance),
                device_id_type=MESH,
            )
            copy.start()
            sent.append(copy)
        copies["rs", q, s] = sent

    def scatter_end(q, s):
        factor_, _, share, _, offset = bases[q][s]
        base = bases[q][s + 1][1]
        for copy in copies["rs", q, s]:
            copy.wait_recv()
        step = block_of(share, 64)
        last = s == stages - 1

        def add(i, _):
            at = rows_of(base + i * step, step)
            value = part[at, :]
            for k in range(factor_[2] - 1):
                value = value + recv[q, rows_of(offset + k * share + i * step, step), :]
            if last:
                full[at, :] = value
            else:
                part[at, :] = value
            return 0

        lax.fori_loop(0, share // step, add, 0)

    def gather_start(q, s):
        factor_, _, share, slot, _ = bases[q][s]
        at = rows_of(bases[q][s + 1][1], share)
        sent = []
        for distance in range(1, factor_[2]):
            copy = pltpu.make_async_remote_copy(
                src_ref=full.at[at],
                dst_ref=full.at[at],
                send_sem=ag_send.at[q, slot + distance - 1],
                recv_sem=ag_recv.at[q, slot + distance - 1],
                device_id=peer_id(factor_, distance),
                device_id_type=MESH,
            )
            copy.start()
            sent.append(copy)
        copies["ag", q, s] = sent

    def gather_end(q, s):
        for copy in copies["ag", q, s]:
            copy.wait_recv()

    depth = math.gcd(rows, 768)

    def project(q):
        def one(i, _):
            at = pl.ds(pl.multiple_of(q * rows + i * depth, 16), depth)
            sketch = full[at, :].T
            high = sketch.astype(BF16)
            rest = sketch - high.astype(F32)
            mid = rest.astype(BF16)
            low = (rest - mid.astype(F32)).astype(BF16)
            parts = jnp.concatenate([high, mid, low], axis=0)
            acc[...] += jnp.dot(parts, values[at, :], preferred_element_type=F32)
            return 0

        lax.fori_loop(0, rows // depth, one, 0)

    def step(q, t):
        if t == 0:
            sketch_piece(q)
            if stages:
                scatter_start(q, 0)
            else:
                full[pl.ds(q * rows, rows), :] = part[pl.ds(q * rows, rows), :]
        elif t < stages:
            scatter_end(q, t - 1)
            scatter_start(q, t)
        elif t == stages:
            scatter_end(q, t - 1)
            gather_start(q, stages - 1)
        elif t < 2 * stages:
            gather_end(q, 2 * stages - t)
            gather_start(q, 2 * stages - t - 1)
        else:
            gather_end(q, 0)
            project(q)

    lanes = plan.lanes
    for time in range(pieces // lanes + 2 * stages):
        for q in range(pieces):
            if 0 <= time - q // lanes <= 2 * stages:
                step(q, time - q // lanes)
    for sent in copies.values():
        for copy in sent:
            copy.wait_send()

    result = acc[:width] + acc[width : 2 * width] + acc[2 * width :]
    total_snps = snps * plan.devices
    for turn in range(2):
        gram[turn] = lax.dot_general(
            result, result, (((1,), (1,)), ((), ())), precision=HIGHEST, preferred_element_type=F32
        )
        value, me, share = sum_gram(plan, turn, gram.at[turn], near, far, sems)
        spread_gram(plan, turn, value, me, share, grams, sems)
        total_gram = grams[turn]
        if turn == 0:
            row = lax.broadcasted_iota(jnp.int32, (width, width), 0)
            lane = lax.broadcasted_iota(jnp.int32, (width, width), 1)
            diagonal = jnp.sum(jnp.where(row == lane, total_gram, 0.0), axis=0, keepdims=True)
            norms_ref[...] = 0.1 * jnp.log(diagonal / total_snps)
        inverse = inverse_factor(total_gram, work)
        result = jnp.dot(inverse, result, precision=HIGHEST, preferred_element_type=F32)
    out_ref[...] = (result * math.sqrt(total_snps)).T


PANEL = 16


def inverse_factor(gram, work):
    width = gram.shape[0]
    row = lax.broadcasted_iota(jnp.int32, (width, width), 0)
    lane = lax.broadcasted_iota(jnp.int32, (width, width), 1)
    work[:, :width] = gram
    work[:, width:] = jnp.where(row == lane, 1.0, 0.0).astype(F32)
    shape = (PANEL, width)
    sub = lax.broadcasted_iota(jnp.int32, shape, 0)
    lanes = lax.broadcasted_iota(jnp.int32, shape, 1)

    def of_row(array, j):
        return jnp.broadcast_to(array[j : j + 1, :], shape)

    for k in range(0, width, PANEL):
        left, right = work[k : k + PANEL, :width], work[k : k + PANEL, width:]
        columns = [jnp.broadcast_to(left[:, k + j : k + j + 1], shape) for j in range(PANEL)]
        scale = jnp.zeros(shape, F32)
        for j in range(PANEL):
            root = lax.rsqrt(of_row(columns[j], j))
            scale = jnp.where(sub == j, root, scale)
            if j < PANEL - 1:
                ratio = jnp.where(sub > j, columns[j] * (root * root), 0.0)
                for m in range(j + 1, PANEL):
                    columns[m] = columns[m] - ratio * of_row(columns[m], j)
                left = left - ratio * of_row(left, j)
                right = right - ratio * of_row(right, j)
        left, right = left * scale, right * scale
        work[k : k + PANEL, width:] = right
        if k + PANEL < width:
            coefficients = jnp.where(lanes >= k + PANEL, left, 0.0).T
            panel = jnp.concatenate([left, right], axis=1)
            work[k + PANEL :, :] -= jnp.dot(
                coefficients[k + PANEL :], panel, precision=HIGHEST, preferred_element_type=F32
            )
    return jnp.where(row >= lane, work[:, width:], 0.0)


def range_basis(plan, genotypes, probes):
    samples, snps = genotypes.shape
    width = probes.shape[1]
    slots = max(1, plan.slots)
    near = max(1, len(plan.near_steps))
    share = width // plan.near_size
    dma = pltpu.SemaphoreType.DMA
    return pl.pallas_call(
        functools.partial(range_kernel, plan),
        out_shape=(
            jax.ShapeDtypeStruct((snps, width), F32),
            jax.ShapeDtypeStruct((1, width), F32),
        ),
        in_specs=[pl.BlockSpec(memory_space=pl.ANY), pl.BlockSpec(memory_space=pltpu.VMEM)],
        out_specs=[pl.BlockSpec(memory_space=pltpu.VMEM)] * 2,
        scratch_shapes=[
            pltpu.VMEM((samples, snps), BF16),
            pltpu.VMEM((samples, width), F32),
            pltpu.VMEM((samples, width), F32),
            pltpu.VMEM((plan.pieces, plan.rows, width), F32),
            pltpu.VMEM((3 * width, snps), F32),
            pltpu.VMEM((2, width, width), F32),
            pltpu.VMEM((2, near, share, width), F32),
            pltpu.VMEM((2, max(1, plan.far_size), share, width), F32),
            pltpu.VMEM((2, width, width), F32),
            pltpu.VMEM((width, 2 * width), F32),
            dma((plan.pieces,)),
        ]
        + [dma((plan.pieces, slots))] * 4
        + [dma((2, near))] * 2
        + [dma((2, max(1, plan.far_slots)))] * 2
        + [dma((2, near))] * 2,
        compiler_params=pltpu.CompilerParams(
            collective_id=0, has_side_effects=True, vmem_limit_bytes=48 * 1024 * 1024
        ),
        name="range_basis",
    )(genotypes, probes)


def body(chroms, snps, genotypes, probes):
    plan = Plan(genotypes.shape[0], chroms, snps)
    unit_basis, norms = range_basis(plan, genotypes, probes)
    return unit_basis, norms.reshape(-1)


def solution(mesh):
    return jax.shard_map(
        functools.partial(body, mesh.shape["chrom"], mesh.shape["snp"]),
        mesh=mesh,
        in_specs=(P(None, AXES), P(AXES, None)),
        out_specs=(P(AXES, None), P()),
        check_vma=False,
    )
```

```python
import functools
import itertools
import math

import jax
import jax.numpy as jnp
from jax import lax
from jax.experimental import pallas as pl
from jax.experimental.pallas import tpu as pltpu
from jax.sharding import PartitionSpec as P

MESH = pl.DeviceIdType.MESH
AXES = ("chrom", "snp")
HIGHEST = lax.Precision.HIGHEST
F32 = jnp.float32
BF16 = jnp.bfloat16


def split_size(size):
    factors = []
    while size > 1:
        factor = 4 if size % 4 == 0 and size > 2 else 2 if size % 2 == 0 else size
        factors.append(factor)
        size //= factor
    return factors


def axis_factors(axis, sizes):
    out, stride = [], 1
    for size in reversed(sizes):
        out.append((axis, stride, size))
        stride *= size
    return out[::-1]


def mesh_factors(chroms, snps):
    halves, rest = [], chroms
    while rest % 2 == 0:
        halves.append(2)
        rest //= 2
    if rest > 1:
        halves.append(rest)
    chrom = axis_factors("chrom", halves)
    core = 2 if snps % 2 == 0 else 1
    snp = [(a, s * core, n) for a, s, n in axis_factors("snp", split_size(snps // core))]
    cores = [("snp", 1, core)] if core > 1 else []
    return cores, chrom, snp


LINK = {"core": 600e3, "far": 50e3}
DELAY = 2.0


def schedule(plan, row_bytes):
    stages = len(plan.factors)
    last = 2 * stages
    free, ready, at, order = {}, {}, [0] * plan.pieces, []
    shares = []
    for q in range(plan.pieces):
        size, path = plan.rows, []
        for factor in plan.order(q):
            size //= factor[2]
            path.append((factor, size))
        shares.append(path)
        ready[q] = 0.0
    now = 0.0
    while any(t <= last for t in at):
        open_ = [q for q in range(plan.pieces) if at[q] <= last]
        there = [q for q in open_ if ready[q] <= now]
        if there:
            q = max(there, key=lambda q: (at[q] != last, at[q], -q))
        else:
            q = min(open_, key=lambda q: (ready[q], q))
        t = at[q]
        if t == 0:
            work = plan.rows * 0.5e-3
        elif t == last:
            work = plan.rows * 0.65e-3
        elif t <= stages:
            work = 0.15 + shares[q][t - 1][1] * row_bytes * 0.2e-6
        else:
            work = 0.1
        now = max(now, ready[q]) + work
        order.append((q, t))
        at[q] = t + 1
        if t < last:
            factor, share = shares[q][t if t < stages else last - 1 - t]
            core = factor in plan.cores
            link = "snp" if factor in plan.snp else factor
            load = factor[2] ** 2 / 4 * share * row_bytes / LINK["core" if core else "far"]
            free[link] = max(now, free.get(link, 0.0)) + load
            ready[q] = free[link] + DELAY
    return order


def coordinate(factor):
    axis, stride, size = factor
    return lax.rem(lax.div(lax.axis_index(axis), stride), size)


def peer_id(factor, distance):
    axis, stride, size = factor
    mine = coordinate(factor)
    other = lax.rem(mine + distance, size)
    return tuple(
        lax.axis_index(a) + (other - mine) * stride if a == axis else lax.axis_index(a)
        for a in AXES
    )


def near_peer(plan, steps):
    ids = {a: lax.axis_index(a) for a in AXES}
    place = 0
    for (axis, stride, size), step in zip(plan.near, steps):
        mine = coordinate((axis, stride, size))
        other = lax.rem(mine + step, size)
        ids[axis] = ids[axis] + (other - mine) * stride
        place = place * size + other
    return tuple(ids[a] for a in AXES), place


def greet(plan):
    barrier = pltpu.get_barrier_semaphore()
    peers = [near_peer(plan, steps)[0] for steps in plan.near_steps]
    for factor in plan.snp:
        peers += [peer_id(factor, distance) for distance in range(1, factor[2])]
    for peer in peers:
        pl.semaphore_signal(barrier, inc=1, device_id=peer, device_id_type=MESH)
    pl.semaphore_wait(barrier, len(peers))


def sum_gram(plan, turn, gram, near, far, sems):
    near_send, near_recv, far_send, far_recv, back_send, back_recv = sems
    share = gram.shape[0] // plan.near_size
    _, me = near_peer(plan, [0] * len(plan.near))
    mine = rows_of(me * share, share)
    copies = []
    for i, steps in enumerate(plan.near_steps):
        peer, place = near_peer(plan, steps)
        copy = pltpu.make_async_remote_copy(
            src_ref=gram.at[rows_of(place * share, share)],
            dst_ref=near.at[turn, i],
            send_sem=near_send.at[turn, i],
            recv_sem=near_recv.at[turn, i],
            device_id=peer,
            device_id_type=MESH,
        )
        copy.start()
        copies.append(copy)
    value = gram[mine, :]
    for i, copy in enumerate(copies):
        copy.wait_recv()
        value = value + near[turn, i]
    pending = list(copies)
    slot, first = 0, 0
    for factor in plan.snp:
        size = factor[2]
        place = first + coordinate(factor)
        far[turn, place] = value
        copies = []
        for distance in range(1, size):
            copy = pltpu.make_async_remote_copy(
                src_ref=far.at[turn, place],
                dst_ref=far.at[turn, place],
                send_sem=far_send.at[turn, slot],
                recv_sem=far_recv.at[turn, slot],
                device_id=peer_id(factor, distance),
                device_id_type=MESH,
            )
            copy.start()
            copies.append(copy)
            slot += 1
        for copy in copies:
            copy.wait_recv()
        value = far[turn, first]
        for k in range(1, size):
            value = value + far[turn, first + k]
        first += size
        pending += copies
    for copy in pending:
        copy.wait_send()
    return value, me, share


def spread_gram(plan, turn, value, me, share, total, sems):
    mine = rows_of(me * share, share)
    total[turn, mine, :] = value
    copies = []
    for i, steps in enumerate(plan.near_steps):
        peer, _ = near_peer(plan, steps)
        copy = pltpu.make_async_remote_copy(
            src_ref=total.at[turn, mine],
            dst_ref=total.at[turn, mine],
            send_sem=sems[4].at[turn, i],
            recv_sem=sems[5].at[turn, i],
            device_id=peer,
            device_id_type=MESH,
        )
        copy.start()
        copies.append(copy)
    for copy in copies:
        copy.wait_recv()
    for copy in copies:
        copy.wait_send()


def rows_of(start, rows):
    return pl.ds(pl.multiple_of(start, 8), rows)


def block_of(rows, most):
    return max(b for b in range(8, most + 1, 8) if rows % b == 0)


class Plan:
    def __init__(self, samples, chroms, snps):
        self.devices = chroms * snps
        per_device = samples // self.devices
        self.pieces = next(q for q in (24, 16, 12, 8, 6, 4, 3, 2, 1) if per_device % (8 * q) == 0)
        self.rows = samples // self.pieces
        self.cores, self.chrom, self.snp = mesh_factors(chroms, snps)
        self.factors = self.cores + self.chrom + self.snp
        self.slots = sum(f[2] - 1 for f in self.factors)
        near = self.cores + [("chrom", 1, chroms)]
        self.near = [f for f in near if f[2] > 1]
        self.near_size = math.prod(f[2] for f in self.near)
        self.near_steps = list(itertools.product(*[range(f[2]) for f in self.near]))[1:]
        self.far_slots = sum(f[2] - 1 for f in self.snp)
        self.far_size = sum(f[2] for f in self.snp)

    def order(self, piece):
        turn = piece % max(1, len(self.chrom))
        return self.cores + self.chrom[turn:] + self.chrom[:turn] + self.snp


def range_kernel(plan, geno_hbm, probes_hbm, out_ref, norms_ref, values, probes_ref, part, full, recv, acc, gram, near, far, grams, work, load_sem, probe_sem, rs_send, rs_recv, ag_send, ag_recv, *sems):
    samples, snps = values.shape
    width = probes_ref.shape[1]
    rows, pieces = plan.rows, plan.pieces
    loads = []
    for q in range(pieces):
        piece = pl.ds(q * rows, rows)
        load = pltpu.make_async_copy(geno_hbm.at[piece], values.at[piece], load_sem.at[q])
        load.start()
        loads.append(load)
    probe_load = pltpu.make_async_copy(probes_hbm, probes_ref, probe_sem)
    probe_load.start()
    greet(plan)

    block = math.gcd(rows, 512)
    zero = jnp.zeros((16, snps), F32)
    sums = (zero, zero)
    for q in range(pieces):
        loads[q].wait()

        def add_block(i, carry, q=q):
            first, second = carry
            start = q * rows + i * block
            one = jnp.zeros((16, snps), BF16)
            two = jnp.zeros((16, snps), BF16)
            for slab in range(block // 16):
                x = values[pl.ds(pl.multiple_of(start + slab * 16, 16), 16), :]
                one = one + x
                two = two + x * x
            return first + one.astype(F32), second + two.astype(F32)

        sums = lax.fori_loop(0, rows // block, add_block, sums)
    total = jnp.sum(sums[0], axis=0, keepdims=True)
    squares = jnp.sum(sums[1], axis=0, keepdims=True)
    mean = total / samples
    whole, square = total.astype(jnp.int32), squares.astype(jnp.int32)
    spread = (square * samples - whole * whole).astype(F32) / float(samples) ** 2
    factor = lax.rsqrt(jnp.sqrt(jnp.sqrt(spread + 1e-05)))
    probe_load.wait()
    probes = probes_ref[...]
    acc[...] = jnp.zeros_like(acc)

    tile = math.gcd(rows, 256)

    def sketch_piece(q):
        def one_tile(i, _):
            at = pl.ds(pl.multiple_of(q * rows + i * tile, 16), tile)
            scaled = ((values[at, :].astype(F32) - mean) * factor).astype(BF16)
            values[at, :] = scaled
            part[at, :] = jnp.dot(scaled, probes, preferred_element_type=F32)
            return 0

        lax.fori_loop(0, rows // tile, one_tile, 0)

    bases = []
    for q in range(pieces):
        base, size, path = q * rows, rows, []
        slot, offset = 0, 0
        for factor_ in plan.order(q):
            share = size // factor_[2]
            path.append((factor_, base, share, slot, offset))
            slot += factor_[2] - 1
            offset += (factor_[2] - 1) * share
            base = base + coordinate(factor_) * share
            size = share
        path.append((None, base, size, slot, offset))
        bases.append(path)
    stages = len(plan.factors)
    copies = {}

    def scatter_start(q, s):
        factor_, base, share, slot, offset = bases[q][s]
        sent = []
        for distance in range(1, factor_[2]):
            other = lax.rem(coordinate(factor_) + distance, factor_[2])
            copy = pltpu.make_async_remote_copy(
                src_ref=part.at[rows_of(base + other * share, share)],
                dst_ref=recv.at[q, pl.ds(offset + (distance - 1) * share, share)],
                send_sem=rs_send.at[q, slot + distance - 1],
                recv_sem=rs_recv.at[q, slot + distance - 1],
                device_id=peer_id(factor_, distance),
                device_id_type=MESH,
            )
            copy.start()
            sent.append(copy)
        copies["rs", q, s] = sent

    def scatter_end(q, s):
        factor_, _, share, _, offset = bases[q][s]
        base = bases[q][s + 1][1]
        for copy in copies["rs", q, s]:
            copy.wait_recv()
        step = block_of(share, 64)
        last = s == stages - 1

        def add(i, _):
            at = rows_of(base + i * step, step)
            value = part[at, :]
            for k in range(factor_[2] - 1):
                value = value + recv[q, rows_of(offset + k * share + i * step, step), :]
            if last:
                full[at, :] = value
            else:
                part[at, :] = value
            return 0

        lax.fori_loop(0, share // step, add, 0)

    def gather_start(q, s):
        factor_, _, share, slot, _ = bases[q][s]
        at = rows_of(bases[q][s + 1][1], share)
        sent = []
        for distance in range(1, factor_[2]):
            copy = pltpu.make_async_remote_copy(
                src_ref=full.at[at],
                dst_ref=full.at[at],
                send_sem=ag_send.at[q, slot + distance - 1],
                recv_sem=ag_recv.at[q, slot + distance - 1],
                device_id=peer_id(factor_, distance),
                device_id_type=MESH,
            )
            copy.start()
            sent.append(copy)
        copies["ag", q, s] = sent

    def gather_end(q, s):
        for copy in copies["ag", q, s]:
            copy.wait_recv()

    depth = block_of(rows, 768)

    def project(q):
        def one(i, _):
            at = pl.ds(pl.multiple_of(q * rows + i * depth, 16), depth)
            sketch = full[at, :].T
            high = sketch.astype(BF16)
            rest = sketch - high.astype(F32)
            mid = rest.astype(BF16)
            low = (rest - mid.astype(F32)).astype(BF16)
            parts = jnp.concatenate([high, mid, low], axis=0)
            acc[...] += jnp.dot(parts, values[at, :], preferred_element_type=F32)
            return 0

        lax.fori_loop(0, rows // depth, one, 0)

    def step(q, t):
        if t == 0:
            sketch_piece(q)
            if stages:
                scatter_start(q, 0)
            else:
                full[pl.ds(q * rows, rows), :] = part[pl.ds(q * rows, rows), :]
        elif t < stages:
            scatter_end(q, t - 1)
            scatter_start(q, t)
        elif t == stages:
            scatter_end(q, t - 1)
            gather_start(q, stages - 1)
        elif t < 2 * stages:
            gather_end(q, 2 * stages - t)
            gather_start(q, 2 * stages - t - 1)
        else:
            gather_end(q, 0)
            project(q)

    for q, t in schedule(plan, width * 4):
        step(q, t)
    for sent in copies.values():
        for copy in sent:
            copy.wait_send()

    result = acc[:width] + acc[width : 2 * width] + acc[2 * width :]
    total_snps = snps * plan.devices
    for turn in range(2):
        gram[turn] = lax.dot_general(
            result, result, (((1,), (1,)), ((), ())), precision=HIGHEST, preferred_element_type=F32
        )
        value, me, share = sum_gram(plan, turn, gram.at[turn], near, far, sems)
        spread_gram(plan, turn, value, me, share, grams, sems)
        total_gram = grams[turn]
        if turn == 0:
            row = lax.broadcasted_iota(jnp.int32, (width, width), 0)
            lane = lax.broadcasted_iota(jnp.int32, (width, width), 1)
            diagonal = jnp.sum(jnp.where(row == lane, total_gram, 0.0), axis=0, keepdims=True)
            norms_ref[...] = 0.1 * jnp.log(diagonal / total_snps)
        inverse = inverse_factor(total_gram, work)
        result = jnp.dot(inverse, result, precision=HIGHEST, preferred_element_type=F32)
    out_ref[...] = (result * math.sqrt(total_snps)).T


PANEL = 16


def inverse_factor(gram, work):
    width = gram.shape[0]
    row = lax.broadcasted_iota(jnp.int32, (width, width), 0)
    lane = lax.broadcasted_iota(jnp.int32, (width, width), 1)
    work[:, :width] = gram
    work[:, width:] = jnp.where(row == lane, 1.0, 0.0).astype(F32)
    following = work[:PANEL, :]
    shape = (PANEL, width)
    sub = lax.broadcasted_iota(jnp.int32, shape, 0)
    lanes = lax.broadcasted_iota(jnp.int32, shape, 1)

    def of_row(array, j):
        return jnp.broadcast_to(array[j : j + 1, :], shape)

    for k in range(0, width, PANEL):
        left, right = following[:, :width], following[:, width:]
        columns = [jnp.broadcast_to(left[:, k + j : k + j + 1], shape) for j in range(PANEL)]
        scale = jnp.zeros(shape, F32)
        for j in range(PANEL):
            root = lax.rsqrt(of_row(columns[j], j))
            scale = jnp.where(sub == j, root, scale)
            if j < PANEL - 1:
                ratio = jnp.where(sub > j, columns[j] * (root * root), 0.0)
                for m in range(j + 1, PANEL):
                    columns[m] = columns[m] - ratio * of_row(columns[m], j)
                left = left - ratio * of_row(left, j)
                right = right - ratio * of_row(right, j)
        left, right = left * scale, right * scale
        work[k : k + PANEL, width:] = right
        if k + PANEL < width:
            coefficients = jnp.where(lanes >= k + PANEL, left, 0.0).T
            panel = jnp.concatenate([left, right], axis=1)
            cut = k + 2 * PANEL
            following = work[k + PANEL : cut, :] - jnp.dot(
                coefficients[k + PANEL : cut], panel, precision=HIGHEST, preferred_element_type=F32
            )
            if cut < width:
                work[cut:, :] -= jnp.dot(
                    coefficients[cut:], panel, precision=HIGHEST, preferred_element_type=F32
                )
    return jnp.where(row >= lane, work[:, width:], 0.0)


def range_basis(plan, genotypes, probes):
    samples, snps = genotypes.shape
    width = probes.shape[1]
    slots = max(1, plan.slots)
    near = max(1, len(plan.near_steps))
    share = width // plan.near_size
    dma = pltpu.SemaphoreType.DMA
    return pl.pallas_call(
        functools.partial(range_kernel, plan),
        out_shape=(
            jax.ShapeDtypeStruct((snps, width), F32),
            jax.ShapeDtypeStruct((1, width), F32),
        ),
        in_specs=[pl.BlockSpec(memory_space=pl.ANY)] * 2,
        out_specs=[pl.BlockSpec(memory_space=pltpu.VMEM)] * 2,
        scratch_shapes=[
            pltpu.VMEM((samples, snps), BF16),
            pltpu.VMEM((snps, width), BF16),
            pltpu.VMEM((samples, width), F32),
            pltpu.VMEM((samples, width), F32),
            pltpu.VMEM((plan.pieces, plan.rows, width), F32),
            pltpu.VMEM((3 * width, snps), F32),
            pltpu.VMEM((2, width, width), F32),
            pltpu.VMEM((2, near, share, width), F32),
            pltpu.VMEM((2, max(1, plan.far_size), share, width), F32),
            pltpu.VMEM((2, width, width), F32),
            pltpu.VMEM((width, 2 * width), F32),
            dma((plan.pieces,)),
            dma(()),
        ]
        + [dma((plan.pieces, slots))] * 4
        + [dma((2, near))] * 2
        + [dma((2, max(1, plan.far_slots)))] * 2
        + [dma((2, near))] * 2,
        compiler_params=pltpu.CompilerParams(
            collective_id=0, has_side_effects=True, vmem_limit_bytes=48 * 1024 * 1024
        ),
        name="range_basis",
    )(genotypes, probes)


def body(chroms, snps, genotypes, probes):
    plan = Plan(genotypes.shape[0], chroms, snps)
    unit_basis, norms = range_basis(plan, genotypes, probes)
    return unit_basis, norms.reshape(-1)


def solution(mesh):
    return jax.shard_map(
        functools.partial(body, mesh.shape["chrom"], mesh.shape["snp"]),
        mesh=mesh,
        in_specs=(P(None, AXES), P(AXES, None)),
        out_specs=(P(AXES, None), P()),
        check_vma=False,
    )
```

```python
import functools
import itertools
import math

import jax
import jax.numpy as jnp
from jax import lax
from jax.experimental import pallas as pl
from jax.experimental.pallas import tpu as pltpu
from jax.sharding import PartitionSpec as P

MESH = pl.DeviceIdType.MESH
AXES = ("chrom", "snp")
HIGHEST = lax.Precision.HIGHEST
F32 = jnp.float32
BF16 = jnp.bfloat16


def split_size(size):
    factors = []
    while size > 1:
        factor = 4 if size % 4 == 0 and size > 2 else 2 if size % 2 == 0 else size
        factors.append(factor)
        size //= factor
    return factors


def axis_factors(axis, sizes):
    out, stride = [], 1
    for size in reversed(sizes):
        out.append((axis, stride, size))
        stride *= size
    return out[::-1]


def mesh_factors(chroms, snps):
    halves, rest = [], chroms
    while rest % 2 == 0:
        halves.append(2)
        rest //= 2
    if rest > 1:
        halves.append(rest)
    chrom = axis_factors("chrom", halves)
    core = 2 if snps % 2 == 0 else 1
    snp = [(a, s * core, n) for a, s, n in axis_factors("snp", split_size(snps // core))]
    cores = [("snp", 1, core)] if core > 1 else []
    return cores, chrom, snp


LINK = {"core": 600e3, "far": 50e3}
DELAY = 2.0


def schedule(plan, row_bytes):
    stages = len(plan.factors)
    last = 2 * stages
    free, ready, at, order = {}, {}, [0] * plan.pieces, []
    shares = []
    for q in range(plan.pieces):
        size, path = plan.rows, []
        for factor in plan.order(q):
            size //= factor[2]
            path.append((factor, size))
        shares.append(path)
        ready[q] = 0.0
    now = 0.0
    while any(t <= last for t in at):
        open_ = [q for q in range(plan.pieces) if at[q] <= last]
        there = [q for q in open_ if ready[q] <= now]
        if there:
            q = max(there, key=lambda q: (at[q] != last, at[q], -q))
        else:
            q = min(open_, key=lambda q: (ready[q], q))
        t = at[q]
        if t == 0:
            work = plan.rows * 0.5e-3
        elif t == last:
            work = plan.rows * 0.65e-3
        elif t <= stages:
            work = 0.15 + shares[q][t - 1][1] * row_bytes * 0.2e-6
        else:
            work = 0.1
        now = max(now, ready[q]) + work
        order.append((q, t))
        at[q] = t + 1
        if t < last:
            factor, share = shares[q][t if t < stages else last - 1 - t]
            core = factor in plan.cores
            link = "snp" if factor in plan.snp else factor
            load = factor[2] ** 2 / 4 * share * row_bytes / LINK["core" if core else "far"]
            free[link] = max(now, free.get(link, 0.0)) + load
            ready[q] = free[link] + DELAY
    return order


def coordinate(factor):
    axis, stride, size = factor
    return lax.rem(lax.div(lax.axis_index(axis), stride), size)


def peer_id(factor, distance):
    axis, stride, size = factor
    mine = coordinate(factor)
    other = lax.rem(mine + distance, size)
    return tuple(
        lax.axis_index(a) + (other - mine) * stride if a == axis else lax.axis_index(a)
        for a in AXES
    )


def near_peer(plan, steps):
    ids = {a: lax.axis_index(a) for a in AXES}
    place = 0
    for (axis, stride, size), step in zip(plan.near, steps):
        mine = coordinate((axis, stride, size))
        other = lax.rem(mine + step, size)
        ids[axis] = ids[axis] + (other - mine) * stride
        place = place * size + other
    return tuple(ids[a] for a in AXES), place


def greet(plan):
    barrier = pltpu.get_barrier_semaphore()
    peers = [near_peer(plan, steps)[0] for steps in plan.near_steps]
    for factor in plan.snp:
        peers += [peer_id(factor, distance) for distance in range(1, factor[2])]
    for peer in peers:
        pl.semaphore_signal(barrier, inc=1, device_id=peer, device_id_type=MESH)
    pl.semaphore_wait(barrier, len(peers))


def sum_gram(plan, turn, gram, near, far, sems):
    near_send, near_recv, far_send, far_recv, back_send, back_recv = sems
    share = gram.shape[0] // plan.near_size
    _, me = near_peer(plan, [0] * len(plan.near))
    mine = rows_of(me * share, share)
    copies = []
    for i, steps in enumerate(plan.near_steps):
        peer, place = near_peer(plan, steps)
        copy = pltpu.make_async_remote_copy(
            src_ref=gram.at[rows_of(place * share, share)],
            dst_ref=near.at[turn, i],
            send_sem=near_send.at[turn, i],
            recv_sem=near_recv.at[turn, i],
            device_id=peer,
            device_id_type=MESH,
        )
        copy.start()
        copies.append(copy)
    value = gram[mine, :]
    for i, copy in enumerate(copies):
        copy.wait_recv()
        value = value + near[turn, i]
    pending = list(copies)
    slot, first = 0, 0
    for factor in plan.snp:
        size = factor[2]
        place = first + coordinate(factor)
        far[turn, place] = value
        copies = []
        for distance in range(1, size):
            copy = pltpu.make_async_remote_copy(
                src_ref=far.at[turn, place],
                dst_ref=far.at[turn, place],
                send_sem=far_send.at[turn, slot],
                recv_sem=far_recv.at[turn, slot],
                device_id=peer_id(factor, distance),
                device_id_type=MESH,
            )
            copy.start()
            copies.append(copy)
            slot += 1
        for copy in copies:
            copy.wait_recv()
        value = far[turn, first]
        for k in range(1, size):
            value = value + far[turn, first + k]
        first += size
        pending += copies
    return value, me, share, pending


def spread_gram(plan, turn, value, me, share, total, sems):
    mine = rows_of(me * share, share)
    total[turn, mine, :] = value
    copies = []
    for i, steps in enumerate(plan.near_steps):
        peer, _ = near_peer(plan, steps)
        copy = pltpu.make_async_remote_copy(
            src_ref=total.at[turn, mine],
            dst_ref=total.at[turn, mine],
            send_sem=sems[4].at[turn, i],
            recv_sem=sems[5].at[turn, i],
            device_id=peer,
            device_id_type=MESH,
        )
        copy.start()
        copies.append(copy)
    for copy in copies:
        copy.wait_recv()
    return copies


def rows_of(start, rows):
    return pl.ds(pl.multiple_of(start, 8), rows)


def block_of(rows, most):
    return max(b for b in range(8, most + 1, 8) if rows % b == 0)


class Plan:
    def __init__(self, samples, chroms, snps):
        self.devices = chroms * snps
        per_device = samples // self.devices
        self.pieces = next(q for q in (24, 16, 12, 8, 6, 4, 3, 2, 1) if per_device % (8 * q) == 0)
        self.rows = samples // self.pieces
        self.cores, self.chrom, self.snp = mesh_factors(chroms, snps)
        self.factors = self.cores + self.chrom + self.snp
        self.slots = sum(f[2] - 1 for f in self.factors)
        near = self.cores + [("chrom", 1, chroms)]
        self.near = [f for f in near if f[2] > 1]
        self.near_size = math.prod(f[2] for f in self.near)
        self.near_steps = list(itertools.product(*[range(f[2]) for f in self.near]))[1:]
        self.far_slots = sum(f[2] - 1 for f in self.snp)
        self.far_size = sum(f[2] for f in self.snp)

    def order(self, piece):
        turn = piece % max(1, len(self.chrom))
        return self.cores + self.chrom[turn:] + self.chrom[:turn] + self.snp


def range_kernel(plan, geno_hbm, probes_hbm, out_ref, norms_ref, values, probes_ref, part, full, recv, acc, gram, near, far, grams, work, load_sem, probe_sem, rs_send, rs_recv, ag_send, ag_recv, *sems):
    samples, snps = values.shape
    width = probes_ref.shape[1]
    rows, pieces = plan.rows, plan.pieces
    loads = []
    for q in range(pieces):
        piece = pl.ds(q * rows, rows)
        load = pltpu.make_async_copy(geno_hbm.at[piece], values.at[piece], load_sem.at[q])
        load.start()
        loads.append(load)
    probe_load = pltpu.make_async_copy(probes_hbm, probes_ref, probe_sem)
    probe_load.start()
    greet(plan)

    block = math.gcd(rows, 512)
    zero = jnp.zeros((16, snps), F32)
    sums = (zero, zero)
    for q in range(pieces):
        loads[q].wait()

        def add_block(i, carry, q=q):
            first, second = carry
            start = q * rows + i * block
            one = jnp.zeros((16, snps), BF16)
            two = jnp.zeros((16, snps), BF16)
            for slab in range(block // 16):
                x = values[pl.ds(pl.multiple_of(start + slab * 16, 16), 16), :]
                one = one + x
                two = two + x * x
            return first + one.astype(F32), second + two.astype(F32)

        sums = lax.fori_loop(0, rows // block, add_block, sums)
    total = jnp.sum(sums[0], axis=0, keepdims=True)
    squares = jnp.sum(sums[1], axis=0, keepdims=True)
    mean = total / samples
    whole, square = total.astype(jnp.int32), squares.astype(jnp.int32)
    spread = (square * samples - whole * whole).astype(F32) / float(samples) ** 2
    factor = lax.rsqrt(jnp.sqrt(jnp.sqrt(spread + 1e-05)))
    probe_load.wait()
    probes = probes_ref[...]
    acc[...] = jnp.zeros_like(acc)

    tile = math.gcd(rows, 256)

    def sketch_piece(q):
        def one_tile(i, _):
            at = pl.ds(pl.multiple_of(q * rows + i * tile, 16), tile)
            scaled = ((values[at, :].astype(F32) - mean) * factor).astype(BF16)
            values[at, :] = scaled
            part[at, :] = jnp.dot(scaled, probes, preferred_element_type=F32)
            return 0

        lax.fori_loop(0, rows // tile, one_tile, 0)

    bases = []
    for q in range(pieces):
        base, size, path = q * rows, rows, []
        slot, offset = 0, 0
        for factor_ in plan.order(q):
            share = size // factor_[2]
            path.append((factor_, base, share, slot, offset))
            slot += factor_[2] - 1
            offset += (factor_[2] - 1) * share
            base = base + coordinate(factor_) * share
            size = share
        path.append((None, base, size, slot, offset))
        bases.append(path)
    stages = len(plan.factors)
    copies = {}

    def scatter_start(q, s):
        factor_, base, share, slot, offset = bases[q][s]
        sent = []
        for distance in range(1, factor_[2]):
            other = lax.rem(coordinate(factor_) + distance, factor_[2])
            copy = pltpu.make_async_remote_copy(
                src_ref=part.at[rows_of(base + other * share, share)],
                dst_ref=recv.at[q, pl.ds(offset + (distance - 1) * share, share)],
                send_sem=rs_send.at[q, slot + distance - 1],
                recv_sem=rs_recv.at[q, slot + distance - 1],
                device_id=peer_id(factor_, distance),
                device_id_type=MESH,
            )
            copy.start()
            sent.append(copy)
        copies["rs", q, s] = sent

    def scatter_end(q, s):
        factor_, _, share, _, offset = bases[q][s]
        base = bases[q][s + 1][1]
        for copy in copies["rs", q, s]:
            copy.wait_recv()
        step = block_of(share, 64)
        last = s == stages - 1

        def add(i, _):
            at = rows_of(base + i * step, step)
            value = part[at, :]
            for k in range(factor_[2] - 1):
                value = value + recv[q, rows_of(offset + k * share + i * step, step), :]
            if last:
                full[at, :] = value
            else:
                part[at, :] = value
            return 0

        lax.fori_loop(0, share // step, add, 0)

    def gather_start(q, s):
        factor_, _, share, slot, _ = bases[q][s]
        at = rows_of(bases[q][s + 1][1], share)
        sent = []
        for distance in range(1, factor_[2]):
            copy = pltpu.make_async_remote_copy(
                src_ref=full.at[at],
                dst_ref=full.at[at],
                send_sem=ag_send.at[q, slot + distance - 1],
                recv_sem=ag_recv.at[q, slot + distance - 1],
                device_id=peer_id(factor_, distance),
                device_id_type=MESH,
            )
            copy.start()
            sent.append(copy)
        copies["ag", q, s] = sent

    def gather_end(q, s):
        for copy in copies["ag", q, s]:
            copy.wait_recv()

    depth = block_of(rows, 768)

    def project(q):
        def one(i, _):
            at = pl.ds(pl.multiple_of(q * rows + i * depth, 16), depth)
            sketch = full[at, :].T
            high = sketch.astype(BF16)
            rest = sketch - high.astype(F32)
            mid = rest.astype(BF16)
            low = (rest - mid.astype(F32)).astype(BF16)
            parts = jnp.concatenate([high, mid, low], axis=0)
            acc[...] += jnp.dot(parts, values[at, :], preferred_element_type=F32)
            return 0

        lax.fori_loop(0, rows // depth, one, 0)

    def step(q, t):
        if t == 0:
            sketch_piece(q)
            if stages:
                scatter_start(q, 0)
            else:
                full[pl.ds(q * rows, rows), :] = part[pl.ds(q * rows, rows), :]
        elif t < stages:
            scatter_end(q, t - 1)
            scatter_start(q, t)
        elif t == stages:
            scatter_end(q, t - 1)
            gather_start(q, stages - 1)
        elif t < 2 * stages:
            gather_end(q, 2 * stages - t)
            gather_start(q, 2 * stages - t - 1)
        else:
            gather_end(q, 0)
            project(q)

    for q, t in schedule(plan, width * 4):
        step(q, t)
    pending = [copy for sent in copies.values() for copy in sent]

    result = acc[:width] + acc[width : 2 * width] + acc[2 * width :]
    total_snps = snps * plan.devices
    for turn in range(2):
        gram[turn] = lax.dot_general(
            result, result, (((1,), (1,)), ((), ())), precision=HIGHEST, preferred_element_type=F32
        )
        value, me, share, sent = sum_gram(plan, turn, gram.at[turn], near, far, sems)
        pending += sent + spread_gram(plan, turn, value, me, share, grams, sems)
        total_gram = grams[turn]
        if turn == 0:
            row = lax.broadcasted_iota(jnp.int32, (width, width), 0)
            lane = lax.broadcasted_iota(jnp.int32, (width, width), 1)
            diagonal = jnp.sum(jnp.where(row == lane, total_gram, 0.0), axis=0, keepdims=True)
            norms_ref[...] = 0.1 * jnp.log(diagonal / total_snps)
        inverse = inverse_factor(total_gram, work)
        result = jnp.dot(inverse, result, precision=HIGHEST, preferred_element_type=F32)
    out_ref[...] = (result * math.sqrt(total_snps)).T
    for copy in pending:
        copy.wait_send()


PANEL = 16


def three_parts(array):
    high = array.astype(BF16).astype(F32)
    rest = array - high
    mid = rest.astype(BF16).astype(F32)
    return high, mid, rest - mid


def inverse_factor(gram, work):
    width = gram.shape[0]
    row = lax.broadcasted_iota(jnp.int32, (width, width), 0)
    lane = lax.broadcasted_iota(jnp.int32, (width, width), 1)
    work[:, :width] = gram
    work[:, width:] = jnp.where(row == lane, 1.0, 0.0).astype(F32)
    following = work[:PANEL, :]
    shape = (PANEL, width)
    sub = lax.broadcasted_iota(jnp.int32, shape, 0)
    lanes = lax.broadcasted_iota(jnp.int32, shape, 1)

    def of_row(array, j):
        return jnp.broadcast_to(array[j : j + 1, :], shape)

    for k in range(0, width, PANEL):
        left, right = following[:, :width], following[:, width:]
        columns = [jnp.broadcast_to(left[:, k + j : k + j + 1], shape) for j in range(PANEL)]
        scale = jnp.zeros(shape, F32)
        for j in range(PANEL):
            root = lax.rsqrt(of_row(columns[j], j))
            scale = jnp.where(sub == j, root, scale)
            if j < PANEL - 1:
                ratio = columns[j] * (root * root)
                for m in range(j + 1, PANEL):
                    columns[m] = columns[m] - ratio * of_row(columns[m], j)
                below = jnp.where(sub > j, ratio, 0.0)
                left = left - below * of_row(left, j)
                right = right - below * of_row(right, j)
        left, right = left * scale, right * scale
        work[k : k + PANEL, width:] = right
        if k + PANEL < width:
            cut = k + 2 * PANEL
            high, mid, low = three_parts(jnp.where(lanes >= k + PANEL, left, 0.0))
            factors = jnp.concatenate([high, high, mid, high, low, mid], axis=0).T.astype(BF16)
            high, mid, low = three_parts(jnp.concatenate([left, right], axis=1))
            panel = jnp.concatenate([high, mid, high, low, high, mid], axis=0).astype(BF16)
            following = work[k + PANEL : cut, :] - jnp.dot(
                factors[k + PANEL : cut], panel, preferred_element_type=F32
            )
            if cut < width:
                work[cut:, :] -= jnp.dot(factors[cut:], panel, preferred_element_type=F32)
    return jnp.where(row >= lane, work[:, width:], 0.0)


def range_basis(plan, genotypes, probes):
    samples, snps = genotypes.shape
    width = probes.shape[1]
    slots = max(1, plan.slots)
    near = max(1, len(plan.near_steps))
    share = width // plan.near_size
    dma = pltpu.SemaphoreType.DMA
    return pl.pallas_call(
        functools.partial(range_kernel, plan),
        out_shape=(
            jax.ShapeDtypeStruct((snps, width), F32),
            jax.ShapeDtypeStruct((1, width), F32),
        ),
        in_specs=[pl.BlockSpec(memory_space=pl.ANY)] * 2,
        out_specs=[pl.BlockSpec(memory_space=pltpu.VMEM)] * 2,
        scratch_shapes=[
            pltpu.VMEM((samples, snps), BF16),
            pltpu.VMEM((snps, width), BF16),
            pltpu.VMEM((samples, width), F32),
            pltpu.VMEM((samples, width), F32),
            pltpu.VMEM((plan.pieces, plan.rows, width), F32),
            pltpu.VMEM((3 * width, snps), F32),
            pltpu.VMEM((2, width, width), F32),
            pltpu.VMEM((2, near, share, width), F32),
            pltpu.VMEM((2, max(1, plan.far_size), share, width), F32),
            pltpu.VMEM((2, width, width), F32),
            pltpu.VMEM((width, 2 * width), F32),
            dma((plan.pieces,)),
            dma(()),
        ]
        + [dma((plan.pieces, slots))] * 4
        + [dma((2, near))] * 2
        + [dma((2, max(1, plan.far_slots)))] * 2
        + [dma((2, near))] * 2,
        compiler_params=pltpu.CompilerParams(
            collective_id=0, has_side_effects=True, vmem_limit_bytes=63 * 1024 * 1024
        ),
        name="range_basis",
    )(genotypes, probes)


def body(chroms, snps, genotypes, probes):
    plan = Plan(genotypes.shape[0], chroms, snps)
    unit_basis, norms = range_basis(plan, genotypes, probes)
    return unit_basis, norms.reshape(-1)


def solution(mesh):
    return jax.shard_map(
        functools.partial(body, mesh.shape["chrom"], mesh.shape["snp"]),
        mesh=mesh,
        in_specs=(P(None, AXES), P(AXES, None)),
        out_specs=(P(AXES, None), P()),
        check_vma=False,
    )
```

```python
import functools
import itertools
import math

import jax
import jax.numpy as jnp
from jax import lax
from jax.experimental import pallas as pl
from jax.experimental.pallas import tpu as pltpu
from jax.sharding import PartitionSpec as P

MESH = pl.DeviceIdType.MESH
AXES = ("chrom", "snp")
HIGHEST = lax.Precision.HIGHEST
F32 = jnp.float32
BF16 = jnp.bfloat16


def split_size(size):
    factors = []
    while size > 1:
        factor = 4 if size % 4 == 0 and size > 2 else 2 if size % 2 == 0 else size
        factors.append(factor)
        size //= factor
    return factors


def axis_factors(axis, sizes):
    out, stride = [], 1
    for size in reversed(sizes):
        out.append((axis, stride, size))
        stride *= size
    return out[::-1]


def mesh_factors(chroms, snps):
    halves, rest = [], chroms
    while rest % 2 == 0:
        halves.append(2)
        rest //= 2
    if rest > 1:
        halves.append(rest)
    chrom = axis_factors("chrom", halves)
    core = 2 if snps % 2 == 0 else 1
    snp = [(a, s * core, n) for a, s, n in axis_factors("snp", split_size(snps // core))]
    cores = [("snp", 1, core)] if core > 1 else []
    return cores, chrom, snp


LINK = {"core": 600e3, "far": 50e3}
DELAY = 1.5


def schedule(plan, row_bytes):
    stages = len(plan.factors)
    last = 2 * stages
    free, ready, at, order = {}, {}, [0] * plan.pieces, []
    shares = []
    for q in range(plan.pieces):
        size, path = plan.rows, []
        for factor in plan.order(q):
            size //= factor[2]
            path.append((factor, size))
        shares.append(path)
        ready[q] = 0.0
    now = 0.0
    while any(t <= last for t in at):
        open_ = [q for q in range(plan.pieces) if at[q] <= last]
        there = [q for q in open_ if ready[q] <= now]
        if there:
            q = max(there, key=lambda q: (at[q] != last, at[q], -q))
        else:
            q = min(open_, key=lambda q: (ready[q], q))
        t = at[q]
        if t == 0:
            work = plan.rows * 0.5e-3
        elif t == last:
            work = plan.rows * 0.65e-3
        elif t <= stages:
            work = 0.15 + shares[q][t - 1][1] * row_bytes * 0.2e-6
        else:
            work = 0.1
        now = max(now, ready[q]) + work
        order.append((q, t))
        at[q] = t + 1
        if t < last:
            factor, share = shares[q][t if t < stages else last - 1 - t]
            core = factor in plan.cores
            link = "snp" if factor in plan.snp else factor
            load = factor[2] ** 2 / 4 * share * row_bytes / LINK["core" if core else "far"]
            free[link] = max(now, free.get(link, 0.0)) + load
            ready[q] = free[link] + DELAY
    return order


def coordinate(factor):
    axis, stride, size = factor
    return lax.rem(lax.div(lax.axis_index(axis), stride), size)


def peer_id(factor, distance):
    axis, stride, size = factor
    mine = coordinate(factor)
    other = lax.rem(mine + distance, size)
    return tuple(
        lax.axis_index(a) + (other - mine) * stride if a == axis else lax.axis_index(a)
        for a in AXES
    )


def near_peer(plan, steps):
    ids = {a: lax.axis_index(a) for a in AXES}
    place = 0
    for (axis, stride, size), step in zip(plan.near, steps):
        mine = coordinate((axis, stride, size))
        other = lax.rem(mine + step, size)
        ids[axis] = ids[axis] + (other - mine) * stride
        place = place * size + other
    return tuple(ids[a] for a in AXES), place


def greet(plan):
    barrier = pltpu.get_barrier_semaphore()
    peers = [near_peer(plan, steps)[0] for steps in plan.near_steps]
    for factor in plan.snp:
        peers += [peer_id(factor, distance) for distance in range(1, factor[2])]
    for peer in peers:
        pl.semaphore_signal(barrier, inc=1, device_id=peer, device_id_type=MESH)
    pl.semaphore_wait(barrier, len(peers))


def sum_gram(plan, turn, gram, near, far, sems):
    near_send, near_recv, far_send, far_recv, back_send, back_recv = sems
    share = gram.shape[0] // plan.near_size
    _, me = near_peer(plan, [0] * len(plan.near))
    mine = rows_of(me * share, share)
    copies = []
    for i, steps in enumerate(plan.near_steps):
        peer, place = near_peer(plan, steps)
        copy = pltpu.make_async_remote_copy(
            src_ref=gram.at[rows_of(place * share, share)],
            dst_ref=near.at[turn, i],
            send_sem=near_send.at[turn, i],
            recv_sem=near_recv.at[turn, i],
            device_id=peer,
            device_id_type=MESH,
        )
        copy.start()
        copies.append(copy)
    value = gram[mine, :]
    for i, copy in enumerate(copies):
        copy.wait_recv()
        value = value + near[turn, i]
    pending = list(copies)
    slot, first = 0, 0
    for factor in plan.snp:
        size = factor[2]
        place = first + coordinate(factor)
        far[turn, place] = value
        copies = []
        for distance in range(1, size):
            copy = pltpu.make_async_remote_copy(
                src_ref=far.at[turn, place],
                dst_ref=far.at[turn, place],
                send_sem=far_send.at[turn, slot],
                recv_sem=far_recv.at[turn, slot],
                device_id=peer_id(factor, distance),
                device_id_type=MESH,
            )
            copy.start()
            copies.append(copy)
            slot += 1
        for copy in copies:
            copy.wait_recv()
        value = far[turn, first]
        for k in range(1, size):
            value = value + far[turn, first + k]
        first += size
        pending += copies
    return value, me, share, pending


def spread_gram(plan, turn, value, me, share, total, sems):
    mine = rows_of(me * share, share)
    total[turn, mine, :] = value
    copies = []
    for i, steps in enumerate(plan.near_steps):
        peer, _ = near_peer(plan, steps)
        copy = pltpu.make_async_remote_copy(
            src_ref=total.at[turn, mine],
            dst_ref=total.at[turn, mine],
            send_sem=sems[4].at[turn, i],
            recv_sem=sems[5].at[turn, i],
            device_id=peer,
            device_id_type=MESH,
        )
        copy.start()
        copies.append(copy)
    for copy in copies:
        copy.wait_recv()
    return copies


def rows_of(start, rows):
    return pl.ds(pl.multiple_of(start, 8), rows)


def block_of(rows, most):
    return max(b for b in range(8, most + 1, 8) if rows % b == 0)


class Plan:
    def __init__(self, samples, chroms, snps):
        self.devices = chroms * snps
        per_device = samples // self.devices
        self.pieces = next(q for q in (16, 12, 8, 6, 4, 3, 2, 1) if per_device % (8 * q) == 0)
        self.rows = samples // self.pieces
        self.cores, self.chrom, self.snp = mesh_factors(chroms, snps)
        self.factors = self.cores + self.chrom + self.snp
        self.slots = sum(f[2] - 1 for f in self.factors)
        near = self.cores + [("chrom", 1, chroms)]
        self.near = [f for f in near if f[2] > 1]
        self.near_size = math.prod(f[2] for f in self.near)
        self.near_steps = list(itertools.product(*[range(f[2]) for f in self.near]))[1:]
        self.far_slots = sum(f[2] - 1 for f in self.snp)
        self.far_size = sum(f[2] for f in self.snp)

    def order(self, piece):
        turn = piece % max(1, len(self.chrom))
        return self.cores + self.chrom[turn:] + self.chrom[:turn] + self.snp


def range_kernel(plan, geno_hbm, probes_hbm, out_ref, norms_ref, values, probes_ref, part, full, recv, acc, gram, near, far, grams, work, load_sem, probe_sem, rs_send, rs_recv, ag_send, ag_recv, *sems):
    samples, snps = values.shape
    width = probes_ref.shape[1]
    rows, pieces = plan.rows, plan.pieces
    loads = []
    for q in range(pieces):
        piece = pl.ds(q * rows, rows)
        load = pltpu.make_async_copy(geno_hbm.at[piece], values.at[piece], load_sem.at[q])
        load.start()
        loads.append(load)
    probe_load = pltpu.make_async_copy(probes_hbm, probes_ref, probe_sem)
    probe_load.start()
    greet(plan)

    block = math.gcd(rows, 512)
    zero = jnp.zeros((16, snps), F32)
    sums = (zero, zero)
    for q in range(pieces):
        loads[q].wait()

        def add_block(i, carry, q=q):
            first, second = carry
            start = q * rows + i * block
            one = jnp.zeros((16, snps), BF16)
            two = jnp.zeros((16, snps), BF16)
            for slab in range(block // 16):
                x = values[pl.ds(pl.multiple_of(start + slab * 16, 16), 16), :]
                one = one + x
                two = two + x * x
            return first + one.astype(F32), second + two.astype(F32)

        sums = lax.fori_loop(0, rows // block, add_block, sums)
    total = jnp.sum(sums[0], axis=0, keepdims=True)
    squares = jnp.sum(sums[1], axis=0, keepdims=True)
    mean = total / samples
    whole, square = total.astype(jnp.int32), squares.astype(jnp.int32)
    spread = (square * samples - whole * whole).astype(F32) / float(samples) ** 2
    factor = lax.rsqrt(jnp.sqrt(jnp.sqrt(spread + 1e-05)))
    probe_load.wait()
    probes = probes_ref[...]
    acc[...] = jnp.zeros_like(acc)

    tile = math.gcd(rows, 256)

    def sketch_piece(q):
        def one_tile(i, _):
            at = pl.ds(pl.multiple_of(q * rows + i * tile, 16), tile)
            scaled = ((values[at, :].astype(F32) - mean) * factor).astype(BF16)
            values[at, :] = scaled
            part[at, :] = jnp.dot(scaled, probes, preferred_element_type=F32)
            return 0

        lax.fori_loop(0, rows // tile, one_tile, 0)

    bases = []
    for q in range(pieces):
        base, size, path = q * rows, rows, []
        slot, offset = 0, 0
        for factor_ in plan.order(q):
            share = size // factor_[2]
            path.append((factor_, base, share, slot, offset))
            slot += factor_[2] - 1
            offset += (factor_[2] - 1) * share
            base = base + coordinate(factor_) * share
            size = share
        path.append((None, base, size, slot, offset))
        bases.append(path)
    stages = len(plan.factors)
    copies = {}

    def scatter_start(q, s):
        factor_, base, share, slot, offset = bases[q][s]
        sent = []
        for distance in range(1, factor_[2]):
            other = lax.rem(coordinate(factor_) + distance, factor_[2])
            copy = pltpu.make_async_remote_copy(
                src_ref=part.at[rows_of(base + other * share, share)],
                dst_ref=recv.at[q, pl.ds(offset + (distance - 1) * share, share)],
                send_sem=rs_send.at[q, slot + distance - 1],
                recv_sem=rs_recv.at[q, slot + distance - 1],
                device_id=peer_id(factor_, distance),
                device_id_type=MESH,
            )
            copy.start()
            sent.append(copy)
        copies["rs", q, s] = sent

    def scatter_end(q, s):
        factor_, _, share, _, offset = bases[q][s]
        base = bases[q][s + 1][1]
        for copy in copies["rs", q, s]:
            copy.wait_recv()
        step = block_of(share, 64)
        last = s == stages - 1

        def add(i, _):
            at = rows_of(base + i * step, step)
            value = part[at, :]
            for k in range(factor_[2] - 1):
                value = value + recv[q, rows_of(offset + k * share + i * step, step), :]
            if last:
                full[at, :] = value
            else:
                part[at, :] = value
            return 0

        lax.fori_loop(0, share // step, add, 0)

    def gather_start(q, s):
        factor_, _, share, slot, _ = bases[q][s]
        at = rows_of(bases[q][s + 1][1], share)
        sent = []
        for distance in range(1, factor_[2]):
            copy = pltpu.make_async_remote_copy(
                src_ref=full.at[at],
                dst_ref=full.at[at],
                send_sem=ag_send.at[q, slot + distance - 1],
                recv_sem=ag_recv.at[q, slot + distance - 1],
                device_id=peer_id(factor_, distance),
                device_id_type=MESH,
            )
            copy.start()
            sent.append(copy)
        copies["ag", q, s] = sent

    def gather_end(q, s):
        for copy in copies["ag", q, s]:
            copy.wait_recv()

    depth = block_of(rows, 768)

    def project(q):
        def one(i, _):
            at = pl.ds(pl.multiple_of(q * rows + i * depth, 16), depth)
            sketch = full[at, :].T
            high = sketch.astype(BF16)
            rest = sketch - high.astype(F32)
            mid = rest.astype(BF16)
            low = (rest - mid.astype(F32)).astype(BF16)
            parts = jnp.concatenate([high, mid, low], axis=0)
            acc[...] += jnp.dot(parts, values[at, :], preferred_element_type=F32)
            return 0

        lax.fori_loop(0, rows // depth, one, 0)

    def step(q, t):
        if t == 0:
            sketch_piece(q)
            if stages:
                scatter_start(q, 0)
            else:
                full[pl.ds(q * rows, rows), :] = part[pl.ds(q * rows, rows), :]
        elif t < stages:
            scatter_end(q, t - 1)
            scatter_start(q, t)
        elif t == stages:
            scatter_end(q, t - 1)
            gather_start(q, stages - 1)
        elif t < 2 * stages:
            gather_end(q, 2 * stages - t)
            gather_start(q, 2 * stages - t - 1)
        else:
            gather_end(q, 0)
            project(q)

    for q, t in schedule(plan, width * 4):
        step(q, t)
    pending = [copy for sent in copies.values() for copy in sent]

    result = acc[:width] + acc[width : 2 * width] + acc[2 * width :]
    total_snps = snps * plan.devices
    for turn in range(2):
        gram[turn] = lax.dot_general(
            result, result, (((1,), (1,)), ((), ())), precision=HIGHEST, preferred_element_type=F32
        )
        value, me, share, sent = sum_gram(plan, turn, gram.at[turn], near, far, sems)
        pending += sent + spread_gram(plan, turn, value, me, share, grams, sems)
        total_gram = grams[turn]
        if turn == 0:
            row = lax.broadcasted_iota(jnp.int32, (width, width), 0)
            lane = lax.broadcasted_iota(jnp.int32, (width, width), 1)
            diagonal = jnp.sum(jnp.where(row == lane, total_gram, 0.0), axis=0, keepdims=True)
            norms_ref[...] = 0.1 * jnp.log(diagonal / total_snps)
        inverse = inverse_factor(total_gram, work)
        result = jnp.dot(inverse, result, precision=HIGHEST, preferred_element_type=F32)
    out_ref[...] = (result * math.sqrt(total_snps)).T
    for copy in pending:
        copy.wait_send()


PANEL = 16


def three_parts(array):
    high = array.astype(BF16).astype(F32)
    rest = array - high
    mid = rest.astype(BF16).astype(F32)
    return high, mid, rest - mid


def inverse_factor(gram, work):
    width = gram.shape[0]
    row = lax.broadcasted_iota(jnp.int32, (width, width), 0)
    lane = lax.broadcasted_iota(jnp.int32, (width, width), 1)
    work[:, :width] = gram
    work[:, width:] = jnp.where(row == lane, 1.0, 0.0).astype(F32)
    following = work[:PANEL, :]
    shape = (PANEL, width)
    sub = lax.broadcasted_iota(jnp.int32, shape, 0)
    lanes = lax.broadcasted_iota(jnp.int32, shape, 1)

    def of_row(array, j):
        return jnp.broadcast_to(array[j : j + 1, :], shape)

    for k in range(0, width, PANEL):
        left, right = following[:, :width], following[:, width:]
        columns = [jnp.broadcast_to(left[:, k + j : k + j + 1], shape) for j in range(PANEL)]
        scale = jnp.zeros(shape, F32)
        for j in range(PANEL):
            root = lax.rsqrt(of_row(columns[j], j))
            scale = jnp.where(sub == j, root, scale)
            if j < PANEL - 1:
                ratio = columns[j] * (root * root)
                for m in range(j + 1, PANEL):
                    columns[m] = columns[m] - ratio * of_row(columns[m], j)
                below = jnp.where(sub > j, ratio, 0.0)
                left = left - below * of_row(left, j)
                right = right - below * of_row(right, j)
        left, right = left * scale, right * scale
        work[k : k + PANEL, width:] = right
        if k + PANEL < width:
            cut = k + 2 * PANEL
            high, mid, low = three_parts(jnp.where(lanes >= k + PANEL, left, 0.0))
            factors = jnp.concatenate([high, high, mid, high, low, mid], axis=0).T.astype(BF16)
            high, mid, low = three_parts(jnp.concatenate([left, right], axis=1))
            panel = jnp.concatenate([high, mid, high, low, high, mid], axis=0).astype(BF16)
            following = work[k + PANEL : cut, :] - jnp.dot(
                factors[k + PANEL : cut], panel, preferred_element_type=F32
            )
            if cut < width:
                work[cut:, :] -= jnp.dot(factors[cut:], panel, preferred_element_type=F32)
    return jnp.where(row >= lane, work[:, width:], 0.0)


def range_basis(plan, genotypes, probes):
    samples, snps = genotypes.shape
    width = probes.shape[1]
    slots = max(1, plan.slots)
    near = max(1, len(plan.near_steps))
    share = width // plan.near_size
    dma = pltpu.SemaphoreType.DMA
    return pl.pallas_call(
        functools.partial(range_kernel, plan),
        out_shape=(
            jax.ShapeDtypeStruct((snps, width), F32),
            jax.ShapeDtypeStruct((1, width), F32),
        ),
        in_specs=[pl.BlockSpec(memory_space=pl.ANY)] * 2,
        out_specs=[pl.BlockSpec(memory_space=pltpu.VMEM)] * 2,
        scratch_shapes=[
            pltpu.VMEM((samples, snps), BF16),
            pltpu.VMEM((snps, width), BF16),
            pltpu.VMEM((samples, width), F32),
            pltpu.VMEM((samples, width), F32),
            pltpu.VMEM((plan.pieces, plan.rows, width), F32),
            pltpu.VMEM((3 * width, snps), F32),
            pltpu.VMEM((2, width, width), F32),
            pltpu.VMEM((2, near, share, width), F32),
            pltpu.VMEM((2, max(1, plan.far_size), share, width), F32),
            pltpu.VMEM((2, width, width), F32),
            pltpu.VMEM((width, 2 * width), F32),
            dma((plan.pieces,)),
            dma(()),
        ]
        + [dma((plan.pieces, slots))] * 4
        + [dma((2, near))] * 2
        + [dma((2, max(1, plan.far_slots)))] * 2
        + [dma((2, near))] * 2,
        compiler_params=pltpu.CompilerParams(
            collective_id=0, has_side_effects=True, vmem_limit_bytes=48 * 1024 * 1024
        ),
        name="range_basis",
    )(genotypes, probes)


def body(chroms, snps, genotypes, probes):
    plan = Plan(genotypes.shape[0], chroms, snps)
    unit_basis, norms = range_basis(plan, genotypes, probes)
    return unit_basis, norms.reshape(-1)


def solution(mesh):
    return jax.shard_map(
        functools.partial(body, mesh.shape["chrom"], mesh.shape["snp"]),
        mesh=mesh,
        in_specs=(P(None, AXES), P(AXES, None)),
        out_specs=(P(AXES, None), P()),
        check_vma=False,
    )
```

```python
import functools
import itertools
import math

import jax
import jax.numpy as jnp
from jax import lax
from jax.experimental import pallas as pl
from jax.experimental.pallas import tpu as pltpu
from jax.sharding import PartitionSpec as P

MESH = pl.DeviceIdType.MESH
AXES = ("chrom", "snp")
HIGHEST = lax.Precision.HIGHEST
F32 = jnp.float32
BF16 = jnp.bfloat16


def split_size(size):
    factors = []
    while size > 1:
        factor = 4 if size % 4 == 0 and size > 2 else 2 if size % 2 == 0 else size
        factors.append(factor)
        size //= factor
    return factors


def axis_factors(axis, sizes):
    out, stride = [], 1
    for size in reversed(sizes):
        out.append((axis, stride, size))
        stride *= size
    return out[::-1]


def mesh_factors(chroms, snps):
    halves, rest = [], chroms
    while rest % 2 == 0:
        halves.append(2)
        rest //= 2
    if rest > 1:
        halves.append(rest)
    chrom = axis_factors("chrom", halves)
    core = 2 if snps % 2 == 0 else 1
    snp = [(a, s * core, n) for a, s, n in axis_factors("snp", split_size(snps // core))]
    cores = [("snp", 1, core)] if core > 1 else []
    return cores, chrom, snp


LINK = {"core": 100e3, "far": 50e3}
DELAY = 1.0


def schedule(plan, row_bytes):
    stages = len(plan.factors)
    last = 2 * stages
    free, ready, at, order = {}, {}, [0] * plan.pieces, []
    shares = []
    for q in range(plan.pieces):
        size, path = plan.rows, []
        for factor in plan.order(q):
            size //= factor[2]
            path.append((factor, size))
        shares.append(path)
        ready[q] = 0.0
    now = 0.0
    while any(t <= last for t in at):
        open_ = [q for q in range(plan.pieces) if at[q] <= last]
        there = [q for q in open_ if ready[q] <= now]
        if there:
            q = max(there, key=lambda q: (at[q] != last, at[q], -q))
        else:
            q = min(open_, key=lambda q: (ready[q], q))
        t = at[q]
        if t == 0:
            work = plan.rows * 0.5e-3
        elif t == last:
            work = plan.rows * 0.65e-3
        elif t <= stages:
            work = 0.15 + shares[q][t - 1][1] * row_bytes * 0.2e-6
        else:
            work = 0.1
        now = max(now, ready[q]) + work
        order.append((q, t))
        at[q] = t + 1
        if t < last:
            factor, share = shares[q][t if t < stages else last - 1 - t]
            core = factor in plan.cores
            link = "snp" if factor in plan.snp else factor
            load = factor[2] ** 2 / 4 * share * row_bytes / LINK["core" if core else "far"]
            free[link] = max(now, free.get(link, 0.0)) + load
            ready[q] = free[link] + DELAY
    return order


def coordinate(factor):
    axis, stride, size = factor
    return lax.rem(lax.div(lax.axis_index(axis), stride), size)


def peer_id(factor, distance):
    axis, stride, size = factor
    mine = coordinate(factor)
    other = lax.rem(mine + distance, size)
    return tuple(
        lax.axis_index(a) + (other - mine) * stride if a == axis else lax.axis_index(a)
        for a in AXES
    )


def near_peer(plan, steps):
    ids = {a: lax.axis_index(a) for a in AXES}
    place = 0
    for (axis, stride, size), step in zip(plan.near, steps):
        mine = coordinate((axis, stride, size))
        other = lax.rem(mine + step, size)
        ids[axis] = ids[axis] + (other - mine) * stride
        place = place * size + other
    return tuple(ids[a] for a in AXES), place


def greet(plan):
    barrier = pltpu.get_barrier_semaphore()
    peers = [near_peer(plan, steps)[0] for steps in plan.near_steps]
    for factor in plan.snp:
        peers += [peer_id(factor, distance) for distance in range(1, factor[2])]
    for peer in peers:
        pl.semaphore_signal(barrier, inc=1, device_id=peer, device_id_type=MESH)
    pl.semaphore_wait(barrier, len(peers))


def sum_gram(plan, turn, gram, near, far, sems):
    near_send, near_recv, far_send, far_recv, back_send, back_recv = sems
    share = gram.shape[0] // plan.near_size
    _, me = near_peer(plan, [0] * len(plan.near))
    mine = rows_of(me * share, share)
    copies = []
    for i, steps in enumerate(plan.near_steps):
        peer, place = near_peer(plan, steps)
        copy = pltpu.make_async_remote_copy(
            src_ref=gram.at[rows_of(place * share, share)],
            dst_ref=near.at[turn, i],
            send_sem=near_send.at[turn, i],
            recv_sem=near_recv.at[turn, i],
            device_id=peer,
            device_id_type=MESH,
        )
        copy.start()
        copies.append(copy)
    value = gram[mine, :]
    for i, copy in enumerate(copies):
        copy.wait_recv()
        value = value + near[turn, i]
    pending = list(copies)
    slot, first = 0, 0
    for factor in plan.snp:
        size = factor[2]
        place = first + coordinate(factor)
        far[turn, place] = value
        copies = []
        for distance in range(1, size):
            copy = pltpu.make_async_remote_copy(
                src_ref=far.at[turn, place],
                dst_ref=far.at[turn, place],
                send_sem=far_send.at[turn, slot],
                recv_sem=far_recv.at[turn, slot],
                device_id=peer_id(factor, distance),
                device_id_type=MESH,
            )
            copy.start()
            copies.append(copy)
            slot += 1
        for copy in copies:
            copy.wait_recv()
        value = far[turn, first]
        for k in range(1, size):
            value = value + far[turn, first + k]
        first += size
        pending += copies
    return value, me, share, pending


def spread_gram(plan, turn, value, me, share, total, sems):
    mine = rows_of(me * share, share)
    total[turn, mine, :] = value
    copies = []
    for i, steps in enumerate(plan.near_steps):
        peer, _ = near_peer(plan, steps)
        copy = pltpu.make_async_remote_copy(
            src_ref=total.at[turn, mine],
            dst_ref=total.at[turn, mine],
            send_sem=sems[4].at[turn, i],
            recv_sem=sems[5].at[turn, i],
            device_id=peer,
            device_id_type=MESH,
        )
        copy.start()
        copies.append(copy)
    for copy in copies:
        copy.wait_recv()
    return copies


def rows_of(start, rows):
    return pl.ds(pl.multiple_of(start, 8), rows)


def block_of(rows, most):
    return max(b for b in range(8, most + 1, 8) if rows % b == 0)


class Plan:
    def __init__(self, samples, chroms, snps):
        self.devices = chroms * snps
        per_device = samples // self.devices
        self.pieces = next(q for q in (24, 16, 12, 8, 6, 4, 3, 2, 1) if per_device % (8 * q) == 0)
        self.rows = samples // self.pieces
        self.cores, self.chrom, self.snp = mesh_factors(chroms, snps)
        self.factors = self.cores + self.chrom + self.snp
        self.slots = sum(f[2] - 1 for f in self.factors)
        near = self.cores + [("chrom", 1, chroms)]
        self.near = [f for f in near if f[2] > 1]
        self.near_size = math.prod(f[2] for f in self.near)
        self.near_steps = list(itertools.product(*[range(f[2]) for f in self.near]))[1:]
        self.far_slots = sum(f[2] - 1 for f in self.snp)
        self.far_size = sum(f[2] for f in self.snp)

    def order(self, piece):
        turn = piece % max(1, len(self.chrom))
        return self.cores + self.chrom[turn:] + self.chrom[:turn] + self.snp


def range_kernel(plan, geno_hbm, probes_hbm, out_ref, norms_ref, values, probes_ref, part, full, recv, acc, gram, near, far, grams, work, load_sem, probe_sem, rs_send, rs_recv, ag_send, ag_recv, *sems):
    samples, snps = values.shape
    width = probes_ref.shape[1]
    rows, pieces = plan.rows, plan.pieces
    loads = []
    for q in range(pieces):
        piece = pl.ds(q * rows, rows)
        load = pltpu.make_async_copy(geno_hbm.at[piece], values.at[piece], load_sem.at[q])
        load.start()
        loads.append(load)
    probe_load = pltpu.make_async_copy(probes_hbm, probes_ref, probe_sem)
    probe_load.start()
    greet(plan)

    block = math.gcd(rows, 512)
    zero = jnp.zeros((16, snps), F32)
    sums = (zero, zero)
    for q in range(pieces):
        loads[q].wait()

        def add_block(i, carry, q=q):
            first, second = carry
            start = q * rows + i * block
            one = jnp.zeros((16, snps), BF16)
            two = jnp.zeros((16, snps), BF16)
            for slab in range(block // 16):
                x = values[pl.ds(pl.multiple_of(start + slab * 16, 16), 16), :]
                one = one + x
                two = two + x * x
            return first + one.astype(F32), second + two.astype(F32)

        sums = lax.fori_loop(0, rows // block, add_block, sums)
    total = jnp.sum(sums[0], axis=0, keepdims=True)
    squares = jnp.sum(sums[1], axis=0, keepdims=True)
    mean = total / samples
    whole, square = total.astype(jnp.int32), squares.astype(jnp.int32)
    spread = (square * samples - whole * whole).astype(F32) / float(samples) ** 2
    factor = lax.rsqrt(jnp.sqrt(jnp.sqrt(spread + 1e-05)))
    probe_load.wait()
    probes = probes_ref[...]
    acc[...] = jnp.zeros_like(acc)

    tile = math.gcd(rows, 256)

    def sketch_piece(q):
        def one_tile(i, _):
            at = pl.ds(pl.multiple_of(q * rows + i * tile, 16), tile)
            scaled = ((values[at, :].astype(F32) - mean) * factor).astype(BF16)
            values[at, :] = scaled
            part[at, :] = jnp.dot(scaled, probes, preferred_element_type=F32)
            return 0

        lax.fori_loop(0, rows // tile, one_tile, 0)

    bases = []
    for q in range(pieces):
        base, size, path = q * rows, rows, []
        slot, offset = 0, 0
        for factor_ in plan.order(q):
            share = size // factor_[2]
            path.append((factor_, base, share, slot, offset))
            slot += factor_[2] - 1
            offset += (factor_[2] - 1) * share
            base = base + coordinate(factor_) * share
            size = share
        path.append((None, base, size, slot, offset))
        bases.append(path)
    stages = len(plan.factors)
    copies = {}

    def scatter_start(q, s):
        factor_, base, share, slot, offset = bases[q][s]
        sent = []
        for distance in range(1, factor_[2]):
            other = lax.rem(coordinate(factor_) + distance, factor_[2])
            copy = pltpu.make_async_remote_copy(
                src_ref=part.at[rows_of(base + other * share, share)],
                dst_ref=recv.at[q, pl.ds(offset + (distance - 1) * share, share)],
                send_sem=rs_send.at[q, slot + distance - 1],
                recv_sem=rs_recv.at[q, slot + distance - 1],
                device_id=peer_id(factor_, distance),
                device_id_type=MESH,
            )
            copy.start()
            sent.append(copy)
        copies["rs", q, s] = sent

    def scatter_end(q, s):
        factor_, _, share, _, offset = bases[q][s]
        base = bases[q][s + 1][1]
        for copy in copies["rs", q, s]:
            copy.wait_recv()
        step = block_of(share, 64)
        last = s == stages - 1

        def add(i, _):
            at = rows_of(base + i * step, step)
            value = part[at, :]
            for k in range(factor_[2] - 1):
                value = value + recv[q, rows_of(offset + k * share + i * step, step), :]
            if last:
                full[at, :] = value
            else:
                part[at, :] = value
            return 0

        lax.fori_loop(0, share // step, add, 0)

    def gather_start(q, s):
        factor_, _, share, slot, _ = bases[q][s]
        at = rows_of(bases[q][s + 1][1], share)
        sent = []
        for distance in range(1, factor_[2]):
            copy = pltpu.make_async_remote_copy(
                src_ref=full.at[at],
                dst_ref=full.at[at],
                send_sem=ag_send.at[q, slot + distance - 1],
                recv_sem=ag_recv.at[q, slot + distance - 1],
                device_id=peer_id(factor_, distance),
                device_id_type=MESH,
            )
            copy.start()
            sent.append(copy)
        copies["ag", q, s] = sent

    def gather_end(q, s):
        for copy in copies["ag", q, s]:
            copy.wait_recv()

    depth = block_of(rows, 768)

    def project(q):
        def one(i, _):
            at = pl.ds(pl.multiple_of(q * rows + i * depth, 16), depth)
            sketch = full[at, :].T
            high = sketch.astype(BF16)
            rest = sketch - high.astype(F32)
            mid = rest.astype(BF16)
            low = (rest - mid.astype(F32)).astype(BF16)
            parts = jnp.concatenate([high, mid, low], axis=0)
            acc[...] += jnp.dot(parts, values[at, :], preferred_element_type=F32)
            return 0

        lax.fori_loop(0, rows // depth, one, 0)

    def step(q, t):
        if t == 0:
            sketch_piece(q)
            if stages:
                scatter_start(q, 0)
            else:
                full[pl.ds(q * rows, rows), :] = part[pl.ds(q * rows, rows), :]
        elif t < stages:
            scatter_end(q, t - 1)
            scatter_start(q, t)
        elif t == stages:
            scatter_end(q, t - 1)
            gather_start(q, stages - 1)
        elif t < 2 * stages:
            gather_end(q, 2 * stages - t)
            gather_start(q, 2 * stages - t - 1)
        else:
            gather_end(q, 0)
            project(q)

    for q, t in schedule(plan, width * 4):
        step(q, t)
    pending = [copy for sent in copies.values() for copy in sent]

    result = acc[:width] + acc[width : 2 * width] + acc[2 * width :]
    total_snps = snps * plan.devices
    for turn in range(2):
        gram[turn] = lax.dot_general(
            result, result, (((1,), (1,)), ((), ())), precision=HIGHEST, preferred_element_type=F32
        )
        value, me, share, sent = sum_gram(plan, turn, gram.at[turn], near, far, sems)
        pending += sent + spread_gram(plan, turn, value, me, share, grams, sems)
        total_gram = grams[turn]
        if turn == 0:
            row = lax.broadcasted_iota(jnp.int32, (width, width), 0)
            lane = lax.broadcasted_iota(jnp.int32, (width, width), 1)
            diagonal = jnp.sum(jnp.where(row == lane, total_gram, 0.0), axis=0, keepdims=True)
            norms_ref[...] = 0.1 * jnp.log(diagonal / total_snps)
        inverse = inverse_factor(total_gram, work)
        result = jnp.dot(inverse, result, precision=HIGHEST, preferred_element_type=F32)
    out_ref[...] = (result * math.sqrt(total_snps)).T
    for copy in pending:
        copy.wait_send()


PANEL = 16


def three_parts(array):
    high = array.astype(BF16).astype(F32)
    rest = array - high
    mid = rest.astype(BF16).astype(F32)
    return high, mid, rest - mid


def inverse_factor(gram, work):
    width = gram.shape[0]
    row = lax.broadcasted_iota(jnp.int32, (width, width), 0)
    lane = lax.broadcasted_iota(jnp.int32, (width, width), 1)
    work[:, :width] = gram
    work[:, width:] = jnp.where(row == lane, 1.0, 0.0).astype(F32)
    following = work[:PANEL, :]
    shape = (PANEL, width)
    sub = lax.broadcasted_iota(jnp.int32, shape, 0)
    lanes = lax.broadcasted_iota(jnp.int32, shape, 1)

    def of_row(array, j):
        return jnp.broadcast_to(array[j : j + 1, :], shape)

    for k in range(0, width, PANEL):
        left, right = following[:, :width], following[:, width:]
        columns = [jnp.broadcast_to(left[:, k + j : k + j + 1], shape) for j in range(PANEL)]
        scale = jnp.zeros(shape, F32)
        for j in range(PANEL):
            root = lax.rsqrt(of_row(columns[j], j))
            scale = jnp.where(sub == j, root, scale)
            if j < PANEL - 1:
                ratio = columns[j] * (root * root)
                for m in range(j + 1, PANEL):
                    columns[m] = columns[m] - ratio * of_row(columns[m], j)
                below = jnp.where(sub > j, ratio, 0.0)
                left = left - below * of_row(left, j)
                right = right - below * of_row(right, j)
        left, right = left * scale, right * scale
        work[k : k + PANEL, width:] = right
        if k + PANEL < width:
            cut = k + 2 * PANEL
            high, mid, low = three_parts(jnp.where(lanes >= k + PANEL, left, 0.0))
            factors = jnp.concatenate([high, high, mid, high, low, mid], axis=0).T.astype(BF16)
            high, mid, low = three_parts(jnp.concatenate([left, right], axis=1))
            panel = jnp.concatenate([high, mid, high, low, high, mid], axis=0).astype(BF16)
            following = work[k + PANEL : cut, :] - jnp.dot(
                factors[k + PANEL : cut], panel, preferred_element_type=F32
            )
            if cut < width:
                work[cut:, :] -= jnp.dot(factors[cut:], panel, preferred_element_type=F32)
    return jnp.where(row >= lane, work[:, width:], 0.0)


def range_basis(plan, genotypes, probes):
    samples, snps = genotypes.shape
    width = probes.shape[1]
    slots = max(1, plan.slots)
    near = max(1, len(plan.near_steps))
    share = width // plan.near_size
    dma = pltpu.SemaphoreType.DMA
    return pl.pallas_call(
        functools.partial(range_kernel, plan),
        out_shape=(
            jax.ShapeDtypeStruct((snps, width), F32),
            jax.ShapeDtypeStruct((1, width), F32),
        ),
        in_specs=[pl.BlockSpec(memory_space=pl.ANY)] * 2,
        out_specs=[pl.BlockSpec(memory_space=pltpu.VMEM)] * 2,
        scratch_shapes=[
            pltpu.VMEM((samples, snps), BF16),
            pltpu.VMEM((snps, width), BF16),
            pltpu.VMEM((samples, width), F32),
            pltpu.VMEM((samples, width), F32),
            pltpu.VMEM((plan.pieces, plan.rows, width), F32),
            pltpu.VMEM((3 * width, snps), F32),
            pltpu.VMEM((2, width, width), F32),
            pltpu.VMEM((2, near, share, width), F32),
            pltpu.VMEM((2, max(1, plan.far_size), share, width), F32),
            pltpu.VMEM((2, width, width), F32),
            pltpu.VMEM((width, 2 * width), F32),
            dma((plan.pieces,)),
            dma(()),
        ]
        + [dma((plan.pieces, slots))] * 4
        + [dma((2, near))] * 2
        + [dma((2, max(1, plan.far_slots)))] * 2
        + [dma((2, near))] * 2,
        compiler_params=pltpu.CompilerParams(
            collective_id=0, has_side_effects=True, vmem_limit_bytes=48 * 1024 * 1024
        ),
        name="range_basis",
    )(genotypes, probes)


def body(chroms, snps, genotypes, probes):
    plan = Plan(genotypes.shape[0], chroms, snps)
    unit_basis, norms = range_basis(plan, genotypes, probes)
    return unit_basis, norms.reshape(-1)


def solution(mesh):
    return jax.shard_map(
        functools.partial(body, mesh.shape["chrom"], mesh.shape["snp"]),
        mesh=mesh,
        in_specs=(P(None, AXES), P(AXES, None)),
        out_specs=(P(AXES, None), P()),
        check_vma=False,
    )
```
